256 devices in a mesh: seq: 64 (over z, x, core), fsdp: 4 (over y).
Axes of the slice: x: 4, y: 4, z: 8, core: 2. Of those that a mesh axis runs over, the one named last changes fastest.
Arguments:
- query_rows: bfloat16 [65536, 2048], P('seq', 'fsdp'), may hold values from -5 to 5
- key_rows: bfloat16 [65536, 2048], P('seq', 'fsdp'), may hold values from -5 to 5
- value_rows: bfloat16 [65536, 2048], P('seq', 'fsdp'), may hold values from -6 to 6
- out_weight: bfloat16 [2048, 4096], P('fsdp'), may hold values from -0.125 to 0.125
- random_ids: int32 [1024, 3], P('seq'), may hold values from 0 to 1023, as said below
- global_ids: int32 [2], replicated, may hold values from 0 to 1023
Outputs:
- mixed: bfloat16 [65536, 4096], P(('seq', 'fsdp'))
The draws below stay inside these ranges and needn't reach their ends.
Inputs may be any that keep to these rules, and one draw needn't show every extreme that they name: `random_ids`: of the 48 ids in the rows of one index of seq, at most 1 lie in the 16 blocks held by any one index of seq, and in every draw some index of seq has exactly 1 of its ids on one index of seq.
All inputs are finite; a program needn't handle non-finite values.
Results may differ from the reference program's by a relative error of at most 0.015.
Values may be sent and summed in bfloat16 or wider, within the bound.
A program may use at most 128 MiB of HBM per device.

```python
import jax
import jax.numpy as jnp
from jax import lax

D = 4096
HEADS = 16
HD = 128
BLOCK = 64
WHALF = 1
G = 2
R = 3
SEQ = 65536
QB_DEV = 16
NB = 1024
CAP = 1
N_SEQ = 64


def drawn_pair(key):
    base = jax.random.fold_in(key, 101)
    first, second = jax.random.split(base, 2)
    shape = (SEQ, HEADS * HD)
    query_part = jax.random.truncated_normal(first, -4.0, 4.0, shape, jnp.float32)
    key_part = jax.random.truncated_normal(second, -4.0, 4.0, shape, jnp.float32)
    return (query_part, key_part)


def draw_query_rows(key, part):
    return drawn_pair(key)[0].astype(jnp.bfloat16)


def draw_key_rows(key, part):
    return drawn_pair(key)[1].astype(jnp.bfloat16)


def draw_random_ids(key, part):
    base = jax.random.fold_in(key, 303)
    heat = jax.random.randint(jax.random.fold_in(base, 7), (N_SEQ,), 0, 4)
    request_count = R * QB_DEV
    pool_size = N_SEQ * CAP

    def one_source(source):
        sub = jax.random.fold_in(base, source + 11)
        first, second, third, fourth = jax.random.split(sub, 4)
        slots = jnp.arange(pool_size)
        owners = slots // CAP
        shuffled = jax.random.permutation(first, pool_size)
        forced = jax.random.randint(second, (), 0, N_SEQ)
        ranking = jnp.where(owners == forced, shuffled - 8 * pool_size, heat[owners] * pool_size + shuffled)
        picked = jnp.argsort(ranking)[:request_count]
        mixing = jax.random.permutation(third, request_count)
        targets = owners[picked][mixing]
        local_ids = jax.random.randint(fourth, (request_count,), 0, QB_DEV)
        return (targets * QB_DEV + local_ids).reshape(QB_DEV, R)
    return jax.vmap(one_source)(jnp.arange(N_SEQ)).reshape(NB, R).astype(jnp.int32)


def steps_of(rng, extent, pieces, low, high):
    level = 1.0
    for dim, shards_of in pieces:
        heights = jax.random.uniform(jax.random.fold_in(jax.random.fold_in(rng, 6), dim), (shards_of,), jnp.float32, low / len(pieces), high / len(pieces))
        level = level * jnp.repeat(jnp.exp(heights), extent[dim] // shards_of).reshape((-1,) + (1,) * (len(extent) - 1 - dim))
    return level


def scatter_about(key, extent, spread, bound, shards=(), kind=jnp.bfloat16):
    result = jax.random.normal(key, extent, jnp.float32) * spread
    if len(shards) > 0:
        result = steps_of(key, extent, shards, -0.22, 0.18) * result
    return jnp.clip(result, min=-bound, max=bound).astype(kind)


def setup_inputs(seed: int = 0) -> dict:
    key_of = jax.random.split(jax.random.key(seed), 7)
    return {
        "query_rows": draw_query_rows(jax.random.fold_in(key_of[6], 71), 0),
        "key_rows": draw_key_rows(jax.random.fold_in(key_of[6], 71), 0),
        "value_rows": scatter_about(key_of[2], (SEQ, HEADS * HD), 1.0, 6.0, ((0, 64), (1, 4))),
        "out_weight": scatter_about(key_of[3], (HEADS * HD, D), (HEADS * HD) ** -0.5, 0.125, ((0, 4),)),
        "random_ids": draw_random_ids(jax.random.fold_in(key_of[6], 71), 0),
        "global_ids": jax.random.randint(key_of[5], (G,), 0, NB).astype(jnp.int32),
    }


masked_value = -1.0e30


def key_table(random_ids, global_ids):
    block_ids = jnp.arange(NB, dtype=jnp.int32)
    offsets = jnp.arange(-WHALF, WHALF + 1, dtype=jnp.int32)
    near_ids = block_ids[:, None] + offsets[None, :]
    inside = (near_ids >= 0) & (near_ids < NB)
    listed = jnp.concatenate([jnp.clip(near_ids, 0, NB - 1).astype(jnp.int32),
                              jnp.broadcast_to(global_ids[None, :], (NB, G)).astype(jnp.int32),
                              random_ids.astype(jnp.int32)], axis=1)
    others = jnp.ones((NB, G + R), dtype=bool)
    key_valid = jnp.concatenate([inside, others], axis=1)
    return listed, key_valid


def reference(query_rows, key_rows, value_rows, out_weight, random_ids, global_ids):
    listed, key_valid = key_table(random_ids, global_ids)
    count_keys = 2 * WHALF + 1 + G + R
    key_blocks = key_rows.reshape(NB, BLOCK, HEADS, HD)
    value_blocks = value_rows.reshape(NB, BLOCK, HEADS, HD)
    query_groups = query_rows.reshape(N_SEQ, QB_DEV, BLOCK, HEADS, HD)
    score_scale = HD ** -0.5

    def attend_group(inputs):
        query_group, list_group, valid_group = inputs
        key_group = key_blocks[list_group].reshape(QB_DEV, count_keys * BLOCK, HEADS, HD)
        value_group = value_blocks[list_group].reshape(QB_DEV, count_keys * BLOCK, HEADS, HD)
        scores = jnp.einsum('qbhd,qkhd->qhbk', query_group.astype(jnp.float32), key_group.astype(jnp.float32)) * score_scale
        key_mask = jnp.repeat(valid_group, BLOCK, axis=1)[:, None, None, :]
        scores = jnp.where(key_mask, scores, masked_value)
        row_max = jnp.max(scores, axis=-1, keepdims=True)
        lifted = jnp.exp(scores - row_max)
        attn_weights = (lifted / jnp.sum(lifted, axis=-1, keepdims=True)).astype(jnp.bfloat16)
        context = jnp.einsum('qhbk,qkhd->qbhd', attn_weights.astype(jnp.float32), value_group.astype(jnp.float32))
        return context.astype(jnp.bfloat16)

    context = lax.map(attend_group, (query_groups,
                                     listed.reshape(N_SEQ, QB_DEV, count_keys),
                                     key_valid.reshape(N_SEQ, QB_DEV, count_keys)))
    context = context.reshape(SEQ, HEADS * HD)
    return jnp.dot(context, out_weight, preferred_element_type=jnp.float32).astype(jnp.bfloat16)
```

```python
import functools

import jax
import jax.numpy as jnp
from jax import lax
from jax.experimental import pallas as pl
from jax.experimental.pallas import tpu as pltpu
from jax.sharding import PartitionSpec as P

HD = 128
BLOCK = 64
G = 2
R = 3
LOW = -1e30
NT = (((1,), (1,)), ((), ()))


def near_kernel(edge_ref, q_ref, k_ref, v_ref, g_ref, acc_ref, max_ref, sum_ref):
    step = pl.program_id(0)
    heads = q_ref.shape[1] // HD
    width = q_ref.shape[1]
    rows = q_ref.shape[0]
    span = rows + 2 * BLOCK
    count = span + G * BLOCK
    row_block = lax.broadcasted_iota(jnp.int32, (rows, count), 0) // BLOCK
    column = lax.broadcasted_iota(jnp.int32, (rows, count), 1)
    key_block = column // BLOCK
    first = edge_ref[0] * jnp.where(step == 0, 1, 0)
    last = edge_ref[1] * jnp.where(step == pl.num_programs(0) - 1, 1, 0)
    near = (key_block >= row_block) & (key_block <= row_block + 2)
    near = near & (key_block >= first) & (key_block < span // BLOCK - last)
    listed = near | (column >= span)
    here = pl.ds(pl.multiple_of(step * rows, rows), span)
    for head in range(heads):
        cols = slice(head * HD, (head + 1) * HD)
        value_cols = slice(width + head * HD, width + (head + 1) * HD)
        keys = jnp.concatenate([k_ref[here, cols], g_ref[:, cols]], axis=0)
        values = jnp.concatenate([v_ref[here, cols], g_ref[:, value_cols]], axis=0)
        scores = lax.dot_general(q_ref[:, cols], keys, NT, preferred_element_type=jnp.float32)
        scores = jnp.where(listed, scores * HD**-0.5, LOW)
        row_max = jnp.max(scores, axis=1, keepdims=True)
        lifted = jnp.exp(scores - row_max)
        row_sum = jnp.sum(lifted, axis=1, keepdims=True)
        acc_ref[:, cols] = jnp.dot(lifted.astype(jnp.bfloat16), values, preferred_element_type=jnp.float32)
        max_ref[:, cols] = jnp.broadcast_to(row_max, (rows, HD))
        sum_ref[:, cols] = jnp.broadcast_to(row_sum, (rows, HD))


def near_part(edges, query, key_pad, value_pad, shared):
    tokens, width = query.shape
    rows = 2 * BLOCK
    whole = lambda array: pl.BlockSpec(array.shape, lambda i, e: (0, 0))
    tile = pl.BlockSpec((rows, width), lambda i, e: (i, 0))
    out = jax.ShapeDtypeStruct((tokens, width), jnp.float32)
    return pl.pallas_call(
        near_kernel,
        grid_spec=pltpu.PrefetchScalarGridSpec(
            num_scalar_prefetch=1,
            grid=(tokens // rows,),
            in_specs=[tile, whole(key_pad), whole(value_pad), whole(shared)],
            out_specs=[tile, tile, tile],
        ),
        out_shape=[out, out, out],
        cost_estimate=pl.CostEstimate(flops=2 * 10**9, bytes_accessed=12 * 10**6, transcendentals=2 * 10**6),
        compiler_params=pltpu.CompilerParams(vmem_limit_bytes=30 << 20),
    )(edges, query, key_pad, value_pad, shared)


def far_kernel(slot_ref, q_ref, acc_ref, max_ref, sum_ref, *rest):
    blocks, out_ref = rest[:-1], rest[-1]
    width = q_ref.shape[1]
    per = q_ref.shape[0] // BLOCK
    for b in range(per):
        rows = slice(b * BLOCK, (b + 1) * BLOCK)
        mine = blocks[b * R : (b + 1) * R]
        for head in range(width // HD):
            cols = slice(head * HD, (head + 1) * HD)
            value_cols = slice(width + head * HD, width + (head + 1) * HD)
            keys = jnp.concatenate([block[0, :, cols] for block in mine], axis=0)
            values = jnp.concatenate([block[0, :, value_cols] for block in mine], axis=0)
            scores = lax.dot_general(q_ref[rows, cols], keys, NT, preferred_element_type=jnp.float32)
            scores = scores * HD**-0.5
            near_max = max_ref[rows, cols]
            row_max = jnp.maximum(jnp.max(scores, axis=1, keepdims=True), near_max)
            lifted = jnp.exp(scores - row_max[:, :1])
            scale = jnp.exp(near_max - row_max)
            row_sum = scale * sum_ref[rows, cols] + jnp.sum(lifted, axis=1, keepdims=True)
            total = scale * acc_ref[rows, cols] + jnp.dot(
                lifted.astype(jnp.bfloat16), values, preferred_element_type=jnp.float32
            )
            out_ref[rows, cols] = (total / row_sum).astype(jnp.bfloat16)


def far_part(slots, query, acc, near_max, near_sum, fetched):
    tokens, width = query.shape
    per = 2
    rows = per * BLOCK
    tile = pl.BlockSpec((rows, width), lambda i, s: (i, 0))

    def pick(j):
        return pl.BlockSpec((1, BLOCK, 2 * width), lambda i, s: (s[i * per * R + j], 0, 0))

    return pl.pallas_call(
        far_kernel,
        grid_spec=pltpu.PrefetchScalarGridSpec(
            num_scalar_prefetch=1,
            grid=(tokens // rows,),
            in_specs=[tile] * 4 + [pick(j) for j in range(per * R)],
            out_specs=tile,
        ),
        out_shape=jax.ShapeDtypeStruct((tokens, width), jnp.bfloat16),
        cost_estimate=pl.CostEstimate(flops=10**9, bytes_accessed=15 * 10**6, transcendentals=10**6),
        compiler_params=pltpu.CompilerParams(vmem_limit_bytes=30 << 20),
    )(slots, query, acc, near_max, near_sum, *([fetched] * (per * R)))


def on_device(query_rows, key_rows, value_rows, out_weight, random_ids, global_ids):
    tokens, width = query_rows.shape
    n = lax.axis_size("seq")
    blocks = tokens // BLOCK
    me = lax.axis_index("seq")
    flat = random_ids.reshape(-1)
    owners, spots = flat // blocks, flat % blocks
    hits = owners[:, None] == jnp.arange(n)[None, :]
    table = jnp.sum(jnp.where(hits, spots[:, None], 0), axis=0)
    wanted = lax.all_to_all(table, "seq", split_axis=0, concat_axis=0, tiled=True)
    pair = jnp.concatenate([key_rows, value_rows], axis=1)
    pair_blocks = pair.reshape(blocks, BLOCK, 2 * width)
    picked = pair_blocks[global_ids % blocks]
    pieces = picked.transpose(1, 0, 2)
    pieces = lax.all_to_all(pieces, "seq", split_axis=0, concat_axis=0, tiled=True)
    piece = pieces[global_ids // blocks, jnp.arange(G)]
    shared = lax.all_gather(piece, "seq", axis=1, tiled=False).reshape(G * BLOCK, 2 * width)
    served = pair_blocks[wanted]
    fetched = lax.all_to_all(served, "seq", split_axis=0, concat_axis=0, tiled=True)
    up = [(i, i + 1) for i in range(n - 1)]
    down = [(j, i) for i, j in up]
    before = lax.ppermute(pair[-BLOCK:], "seq", up)
    after = lax.ppermute(pair[:BLOCK], "seq", down)
    padded = jnp.concatenate([before, pair, after], axis=0)
    edges = jnp.stack([me == 0, me == n - 1]).astype(jnp.int32)
    acc, near_max, near_sum = near_part(edges, query_rows, padded[:, :width], padded[:, width:], shared)
    context = far_part(owners, query_rows, acc, near_max, near_sum, fetched)
    all_heads = lax.all_to_all(context, "fsdp", split_axis=0, concat_axis=1, tiled=True)
    weight = lax.all_gather(out_weight, "fsdp", axis=0, tiled=True)
    return jnp.dot(all_heads, weight, preferred_element_type=jnp.float32).astype(jnp.bfloat16)


def solution(mesh):
    return jax.shard_map(
        on_device,
        mesh=mesh,
        in_specs=(
            P("seq", "fsdp"),
            P("seq", "fsdp"),
            P("seq", "fsdp"),
            P("fsdp", None),
            P("seq", None),
            P(),
        ),
        out_specs=P(("seq", "fsdp"), None),
        check_vma=False,
    )
```

```python
import jax
import jax.numpy as jnp
from jax import lax
from jax.experimental import pallas as pl
from jax.experimental.pallas import tpu as pltpu
from jax.sharding import PartitionSpec as P

HD = 128
BLOCK = 64
G = 2
R = 3
LOW = -1e30
NT = (((1,), (1,)), ((), ()))
MESH = pl.DeviceIdType.MESH
PLANE = 8
LAYERS = 8
SHIFTS = (0, 1, -1, 2, -2, 3, -3, 4)


def lanes_of(parts):
    rows = parts[0].shape[0]
    lane = lax.broadcasted_iota(jnp.int32, (rows, HD), 1)
    out = jnp.zeros((rows, HD), jnp.float32)
    for i, part in enumerate(parts):
        out = jnp.where(lane == i, part, out)
    return out


def kernel(
    table, inverse, owners, flags, keep,
    q_ref, k_ref, v_ref,
    heads_ref,
    fetched, front1, back1, front2, back2, stage, pick3, got3, got4,
    halo, key_pad, value_pad, g_mine, g_in, g_part, g_col, g_sum, g_all,
    near_acc, near_max, near_sum, far_acc, far_max, far_sum, context,
    hop1_s, hop1_r, hop2_s, hop2_r, hop3_s, hop3_r, hop4_s, hop4_r,
    in_s, in_r, halo_s, halo_r, g_s, g_r, c_s, c_r,
):
    me = lax.axis_index("seq")
    row = lax.axis_index("fsdp")
    z, p_me = me // PLANE, me % PLANE
    count = PLANE * LAYERS
    tokens, width = key_pad.shape[0] - 2 * BLOCK, q_ref.shape[2]
    heads = width // HD
    pair = 2 * BLOCK

    def col(shift):
        return lax.rem(z + shift + LAYERS, LAYERS) * PLANE + p_me

    def mate(r):
        return lax.rem(p_me + r, PLANE)

    def from_mate(r):
        return lax.rem(p_me - r + PLANE, PLANE)

    def layer(d):
        return lax.rem(z - SHIFTS[d] + LAYERS, LAYERS)

    def copy(src, dst, send, recv, device):
        return pltpu.make_async_remote_copy(
            src_ref=src, dst_ref=dst, send_sem=send, recv_sem=recv,
            device_id={"seq": device}, device_id_type=MESH,
        )

    def cross(src, dst, send, recv, device):
        return pltpu.make_async_remote_copy(
            src_ref=src, dst_ref=dst, send_sem=send, recv_sem=recv,
            device_id={"fsdp": device}, device_id_type=MESH,
        )

    next_one, last_one = lax.rem(me + 1, count), lax.rem(me + count - 1, count)
    barrier = pltpu.get_barrier_semaphore()
    for r in range(1, PLANE):
        pl.semaphore_signal(barrier, inc=1, device_id={"seq": z * PLANE + mate(r)}, device_id_type=MESH)
    for s in range(1, LAYERS):
        pl.semaphore_signal(barrier, inc=1, device_id={"seq": col(s)}, device_id_type=MESH)
    pl.semaphore_signal(barrier, inc=1, device_id={"seq": next_one}, device_id_type=MESH)
    pl.semaphore_signal(barrier, inc=1, device_id={"seq": last_one}, device_id_type=MESH)
    for f in range(1, 4):
        pl.semaphore_signal(barrier, inc=1, device_id={"fsdp": lax.rem(row + f, 4)}, device_id_type=MESH)
    pl.semaphore_wait(barrier, 7 + 7 + 2 + 3)

    ways = (1, -1)
    first_hop, second_hop = (front1, back1), (front2, back2)
    own = (k_ref, v_ref)

    def hop1(w, t):
        return copy(own[t], first_hop[w].at[t], hop1_s.at[w, t], hop1_r.at[w, t], col(ways[w]))

    def hop2(w, t):
        return copy(first_hop[w].at[t], second_hop[w].at[t], hop2_s.at[w, t], hop2_r.at[w, t], col(ways[w]))

    def hop3(w, c):
        part = pl.ds(0, 4) if c == 0 else pl.ds(2 * c + 2, 2)
        return copy(pick3.at[w, part], got3.at[w, part], hop3_s.at[w, c], hop3_r.at[w, c], col(ways[w]))

    def hop4(w):
        return copy(got3.at[w, pl.ds(0, 4)], got4.at[w], hop4_s.at[w], hop4_r.at[w], col(ways[w]))

    for t in range(2):
        for w in range(2):
            hop1(w, t).start()

    def halo_copy(side, t):
        block = tokens // BLOCK - 1 if side == 0 else 0
        return copy(
            own[t].at[block], halo.at[side, pl.ds(t * BLOCK, BLOCK)], halo_s.at[side, t], halo_r.at[side, t],
            next_one if side == 0 else last_one,
        )

    for side in range(2):
        for t in range(2):
            halo_copy(side, t).start()

    piece = G * pair // PLANE
    for g in range(G):
        for t in range(2):
            block = own[t][flags[g]].astype(jnp.float32) * keep[g]
            g_mine[pl.ds(g * pair + t * BLOCK, BLOCK), :] = block.astype(jnp.bfloat16)

    def piece_at(p):
        return pl.ds(pl.multiple_of(p * piece, piece), piece)

    def g1(r, p):
        return copy(g_mine.at[piece_at(p)], g_in.at[r], g_s.at[0, r], g_r.at[0, r], z * PLANE + p)

    def g2(s):
        return copy(g_part, g_col.at[s], g_s.at[1, s], g_r.at[1, s], col(s))

    def g3(r, p, at):
        return copy(g_sum, g_all.at[piece_at(at)], g_s.at[2, r], g_r.at[2, r], z * PLANE + p)

    def each(low, high, body):
        def step(i, carry):
            body(i)
            return carry

        lax.fori_loop(low, high, step, 0)

    each(1, PLANE, lambda r: g1(r, mate(r)).start())
    g_in[0] = g_mine[piece_at(p_me), :]

    def choose(d, source):
        owner = layer(d) * PLANE + p_me

        def one(r):
            spot = table[z * PLANE + mate(r), owner]
            for t in range(2):
                stage[d, r, pl.ds(t * BLOCK, BLOCK), :] = source(t, spot)

        each(0, PLANE, one)
        fetched[owner] = stage[d, 0]

    def spread_one(d, r, src):
        owner = layer(d) * PLANE + p_me
        return copy(src, fetched.at[owner], in_s.at[d, r], in_r.at[d, r], z * PLANE + mate(r))

    def spread(d):
        each(1, PLANE, lambda r: spread_one(d, r, stage.at[d, r]).start())

    def arrived(d, r):
        owner = layer(d) * PLANE + from_mate(r)
        copy(fetched.at[owner], fetched.at[owner], in_s.at[d, r], in_r.at[d, r], z * PLANE + mate(r)).wait_recv()

    def columns(h):
        return pl.ds(h * HD, HD)

    def attend(owner):
        asker = inverse[owner]
        scores = []
        for h in range(heads):
            keys = fetched[owner, pl.ds(0, BLOCK), columns(h)]
            scores.append(lax.dot_general(q_ref[asker, :, columns(h)], keys, NT, preferred_element_type=jnp.float32))
        scores = jnp.concatenate(scores, axis=0) * HD**-0.5
        row_max = jnp.max(scores, axis=1, keepdims=True)
        lifted = jnp.exp(scores - row_max)
        row_sum = jnp.sum(lifted, axis=1, keepdims=True)
        lifted = lifted.astype(jnp.bfloat16)
        parts = [slice(h * BLOCK, (h + 1) * BLOCK) for h in range(heads)]
        for h in range(heads):
            values = fetched[owner, pl.ds(BLOCK, BLOCK), columns(h)]
            far_acc[owner, :, columns(h)] = jnp.dot(lifted[parts[h]], values, preferred_element_type=jnp.float32)
        far_max[owner] = lanes_of([row_max[part] for part in parts])
        far_sum[owner] = lanes_of([row_sum[part] for part in parts])

    def attend_layer(d):
        def one(r):
            @pl.when(r > 0)
            def _():
                arrived(d, r)

            attend(layer(d) * PLANE + from_mate(r))

        each(0, PLANE, one)

    choose(0, lambda t, spot: own[t][spot])
    spread(0)

    each(1, PLANE, lambda r: g1(r, mate(r)).wait_recv())
    total = g_in[0]
    for r in range(1, PLANE):
        total = total + g_in[r]
    g_part[...] = total
    each(1, LAYERS, lambda s: g2(s).start())
    g_col[0] = total

    attend_layer(0)

    for t in range(2):
        for w in range(2):
            hop1(w, t).wait_recv()
            hop2(w, t).start()
    for w in range(2):
        choose(1 + w, lambda t, spot: first_hop[w][t, spot])
        spread(1 + w)

    each(1, LAYERS, lambda s: g2(s).wait_recv())
    total = g_col[0]
    for s in range(1, LAYERS):
        total = total + g_col[s]
    g_sum[...] = total
    each(1, PLANE, lambda r: g3(r, mate(r), p_me).start())
    g_all[piece_at(p_me), :] = total

    for side in range(2):
        for t in range(2):
            halo_copy(side, t).wait_recv()
    pads = (key_pad, value_pad)
    for t in range(2):
        pads[t][pl.ds(0, BLOCK), :] = halo[0, pl.ds(t * BLOCK, BLOCK), :]
        pads[t][pl.ds(BLOCK, tokens), :] = own[t][...].reshape(tokens, width)
        pads[t][pl.ds(BLOCK + tokens, BLOCK), :] = halo[1, pl.ds(t * BLOCK, BLOCK), :]
    each(1, PLANE, lambda r: g3(r, mate(r), from_mate(r)).wait_recv())

    tile = 2 * BLOCK
    span = tile + 2 * BLOCK
    steps = tokens // tile

    def near(step):
        wide = span + G * BLOCK
        row_block = lax.broadcasted_iota(jnp.int32, (tile, wide), 0) // BLOCK
        column = lax.broadcasted_iota(jnp.int32, (tile, wide), 1)
        key_block = column // BLOCK
        first = jnp.where((me == 0) & (step == 0), 1, 0)
        last = jnp.where((me == count - 1) & (step == steps - 1), 1, 0)
        listed = (key_block >= row_block) & (key_block <= row_block + 2)
        listed = listed & (key_block >= first) & (key_block < span // BLOCK - last)
        listed = listed | (column >= span)
        rows = pl.ds(pl.multiple_of(step * tile, tile), tile)
        around = pl.ds(pl.multiple_of(step * tile, tile), span)
        maxima, sums = [], []
        for h in range(heads):
            shared = [g_all[pl.ds(b * BLOCK, BLOCK), columns(h)] for b in range(2 * G)]
            keys = jnp.concatenate([key_pad[around, columns(h)]] + shared[0::2], axis=0)
            values = jnp.concatenate([value_pad[around, columns(h)]] + shared[1::2], axis=0)
            query = q_ref[pl.ds(step * (tile // BLOCK), tile // BLOCK), :, columns(h)].reshape(tile, HD)
            scores = lax.dot_general(query, keys, NT, preferred_element_type=jnp.float32)
            scores = jnp.where(listed, scores * HD**-0.5, LOW)
            row_max = jnp.max(scores, axis=1, keepdims=True)
            lifted = jnp.exp(scores - row_max)
            maxima.append(row_max)
            sums.append(jnp.sum(lifted, axis=1, keepdims=True))
            near_acc[rows, columns(h)] = jnp.dot(
                lifted.astype(jnp.bfloat16), values, preferred_element_type=jnp.float32
            )
        near_max[rows, :] = lanes_of(maxima)
        near_sum[rows, :] = lanes_of(sums)

    each(0, steps, near)
    for w in range(2):
        attend_layer(1 + w)

    for w in range(2):
        for t in range(2):
            hop2(w, t).wait_recv()
        way = ways[w]
        owner = col(-2 * way)

        def one(j, r, far):
            to = lax.rem(z + far * way + LAYERS, LAYERS) * PLANE + mate(r)
            spot = table[to, owner]
            for t in range(2):
                pick3[w, j, pl.ds(t * BLOCK, BLOCK), :] = second_hop[w][t, spot]

        each(0, 4, lambda j: one(j, 2 * j + w, 2))
        each(0, PLANE, lambda r: one(4 + r, r, 1))
        for c in range(5):
            hop3(w, c).start()
    for w in range(2):
        choose(3 + w, lambda t, spot: second_hop[w][t, spot])
        spread(3 + w)
    for w in range(2):
        hop3(w, 0).wait_recv()
        hop4(w).start()
    for c in range(1, 5):
        for w in range(2):
            hop3(w, c).wait_recv()
            for r in (2 * c - 2, 2 * c - 1):
                if r == 0:
                    fetched[layer(5 + w) * PLANE + p_me] = got3[w, 4]
                else:
                    spread_one(5 + w, r, got3.at[w, 4 + r]).start()
        if c <= 2:
            attend_layer(2 + c)
    for w in range(2):
        hop4(w).wait_recv()
    for r in range(PLANE):
        if r == 0:
            fetched[layer(7) * PLANE + p_me] = got4[0, 0]
        else:
            spread_one(7, r, got4.at[r % 2, r // 2]).start()
    attend_layer(5)
    attend_layer(6)
    attend_layer(7)

    quarter = tokens // 4

    def merge(block):
        rows = pl.ds(pl.multiple_of(block * BLOCK, BLOCK), BLOCK)
        slots = [owners[block * R + j] for j in range(R)]
        maxima = [near_max[rows, :]] + [far_max[slot] for slot in slots]
        top = maxima[0]
        for one in maxima[1:]:
            top = jnp.maximum(top, one)
        scales = [jnp.exp(one - top) for one in maxima]
        sums = [near_sum[rows, :]] + [far_sum[slot] for slot in slots]
        whole = scales[0] * sums[0]
        for scale, one in zip(scales[1:], sums[1:]):
            whole = whole + scale * one
        scales = [scale / whole for scale in scales]
        for h in range(heads):
            out = scales[0][:, h : h + 1] * near_acc[rows, columns(h)]
            for scale, slot in zip(scales[1:], slots):
                out = out + scale[:, h : h + 1] * far_acc[slot, :, columns(h)]
            context[rows, columns(h)] = out.astype(jnp.bfloat16)

    def quarter_at(f):
        return pl.ds(pl.multiple_of(f * quarter, quarter), quarter)

    def heads_at(f):
        return pl.ds(pl.multiple_of(f * width, width), width)

    blocks = quarter // BLOCK
    for f in (2, 1, 3, 0):
        to = lax.rem(row + f, 4)
        each(0, blocks, lambda b: merge(to * blocks + b))
        if f > 0:
            cross(context.at[quarter_at(to)], heads_ref.at[:, heads_at(row)], c_s.at[f], c_r.at[f], to).start()
        else:
            heads_ref[:, heads_at(row)] = context[quarter_at(row), :]

    for t in range(2):
        for w in range(2):
            hop1(w, t).wait_send()
            hop2(w, t).wait_send()
    for w in range(2):
        for c in range(5):
            hop3(w, c).wait_send()
        hop4(w).wait_send()
    for side in range(2):
        for t in range(2):
            halo_copy(side, t).wait_send()
    for d in range(LAYERS):
        each(1, PLANE, lambda r: spread_one(d, r, fetched.at[0]).wait_send())
    each(1, PLANE, lambda r: g1(r, mate(r)).wait_send())
    each(1, LAYERS, lambda s: g2(s).wait_send())
    each(1, PLANE, lambda r: g3(r, mate(r), p_me).wait_send())
    for f in range(1, 4):
        cross(context.at[quarter_at(0)], heads_ref.at[:, heads_at(row)], c_s.at[f], c_r.at[f], row).wait_send()
        came = lax.rem(row - f + 4, 4)
        cross(context.at[quarter_at(0)], heads_ref.at[:, heads_at(came)], c_s.at[f], c_r.at[f], row).wait_recv()


def gather_attend(table, inverse, owners, flags, keep, query, keys, values):
    tokens, width = query.shape[0] * BLOCK, query.shape[2]
    n = table.shape[0]
    pair = 2 * BLOCK
    piece = G * pair // PLANE
    half, full = jnp.bfloat16, jnp.float32
    vmem = pl.BlockSpec(memory_space=pltpu.VMEM)
    smem = pl.BlockSpec(memory_space=pltpu.SMEM)
    sem = pltpu.SemaphoreType.DMA
    hop = pltpu.VMEM((2,) + query.shape, half)
    return pl.pallas_call(
        kernel,
        out_shape=jax.ShapeDtypeStruct((tokens // 4, 4 * width), half),
        in_specs=[smem] * 5 + [vmem] * 3,
        out_specs=vmem,
        scratch_shapes=[
            pltpu.VMEM((n, pair, width), half),
            hop, hop, hop, hop,
            pltpu.VMEM((5, PLANE, pair, width), half),
            pltpu.VMEM((2, 12, pair, width), half),
            pltpu.VMEM((2, 12, pair, width), half),
            pltpu.VMEM((2, 4, pair, width), half),
            pltpu.VMEM((2, pair, width), half),
            pltpu.VMEM((tokens + pair, width), half),
            pltpu.VMEM((tokens + pair, width), half),
            pltpu.VMEM((G * pair, width), half),
            pltpu.VMEM((PLANE, piece, width), half),
            pltpu.VMEM((piece, width), half),
            pltpu.VMEM((LAYERS, piece, width), half),
            pltpu.VMEM((piece, width), half),
            pltpu.VMEM((G * pair, width), half),
            pltpu.VMEM((tokens, width), full),
            pltpu.VMEM((tokens, HD), full),
            pltpu.VMEM((tokens, HD), full),
            pltpu.VMEM((n, BLOCK, width), full),
            pltpu.VMEM((n, BLOCK, HD), full),
            pltpu.VMEM((n, BLOCK, HD), full),
            pltpu.VMEM((tokens, width), half),
            sem((2, 2)), sem((2, 2)), sem((2, 2)), sem((2, 2)),
            sem((2, 5)), sem((2, 5)), sem((2,)), sem((2,)),
            sem((LAYERS, PLANE)), sem((LAYERS, PLANE)),
            sem((2, 2)), sem((2, 2)), sem((3, 8)), sem((3, 8)), sem((4,)), sem((4,)),
        ],
        compiler_params=pltpu.CompilerParams(
            collective_id=0, has_side_effects=True, vmem_limit_bytes=58 << 20
        ),
        cost_estimate=pl.CostEstimate(flops=3 * 10**9, bytes_accessed=10 * 10**6, transcendentals=4 * 10**6),
    )(table, inverse, owners, flags, keep, query, keys, values)


def on_device(query_rows, key_rows, value_rows, out_weight, random_ids, global_ids):
    tokens, width = query_rows.shape
    n = lax.axis_size("seq")
    blocks = tokens // BLOCK
    me = lax.axis_index("seq")
    flat = random_ids.reshape(-1)
    owners, spots = flat // blocks, flat % blocks
    hits = owners[:, None] == jnp.arange(n)[None, :]
    mine = jnp.sum(jnp.where(hits, spots[:, None], 0), axis=0)
    inverse = jnp.sum(jnp.where(hits, (jnp.arange(flat.shape[0]) // R)[:, None], 0), axis=0)
    table = lax.all_to_all(
        jnp.broadcast_to(mine[None], (n, n)), "seq", split_axis=0, concat_axis=0, tiled=True
    )
    flags = global_ids % blocks
    keep = (global_ids // blocks == me).astype(jnp.float32)
    weight = lax.all_gather(out_weight, "fsdp", axis=0, tiled=True)
    rows = [array.reshape(blocks, BLOCK, width) for array in (query_rows, key_rows, value_rows)]
    all_heads = gather_attend(table, inverse, owners, flags, keep, *rows)
    return jnp.dot(all_heads, weight, preferred_element_type=jnp.float32).astype(jnp.bfloat16)


def solution(mesh):
    return jax.shard_map(
        on_device,
        mesh=mesh,
        in_specs=(
            P("seq", "fsdp"),
            P("seq", "fsdp"),
            P("seq", "fsdp"),
            P("fsdp", None),
            P("seq", None),
            P(),
        ),
        out_specs=P(("seq", "fsdp"), None),
        check_vma=False,
    )
```

```python
import jax
import jax.numpy as jnp
from jax import lax
from jax.experimental import pallas as pl
from jax.experimental.pallas import tpu as pltpu
from jax.sharding import PartitionSpec as P

HD = 128
BLOCK = 64
G = 2
R = 3
LOW = -1e30
NT = (((1,), (1,)), ((), ()))
MESH = pl.DeviceIdType.MESH
PLANE = 8
LAYERS = 8
SHIFTS = (0, 1, -1, 2, -2, 3, -3, 4)


def lanes_of(parts):
    rows = parts[0].shape[0]
    lane = lax.broadcasted_iota(jnp.int32, (rows, HD), 1)
    out = jnp.zeros((rows, HD), jnp.float32)
    for i, part in enumerate(parts):
        out = jnp.where(lane == i, part, out)
    return out


def kernel(
    ids, shared_ids,
    q_ref, k_ref, v_ref,
    heads_ref,
    fetched, front1, back1, front2, back2, stage, pick3, got3, got4,
    halo, key_pad, value_pad, g_mine, g_in, g_part, g_col, g_sum, g_all,
    near_acc, near_max, near_sum, far_acc, far_max, far_sum, context,
    mine_v, inverse_v, table_v, tables_v, inverse, table, tables,
    hop1_s, hop1_r, hop2_s, hop2_r, hop3_s, hop3_r, hop4_s, hop4_r,
    in_s, in_r, halo_s, halo_r, g_s, g_r, c_s, c_r, t_s, t_r, far_s, far_r, local_s,
):
    me = lax.axis_index("seq")
    row = lax.axis_index("fsdp")
    z, p_me = me // PLANE, me % PLANE
    count = PLANE * LAYERS
    tokens, width = key_pad.shape[0] - 2 * BLOCK, q_ref.shape[2]
    heads = width // HD
    pair = 2 * BLOCK

    def col(shift):
        return lax.rem(z + shift + LAYERS, LAYERS) * PLANE + p_me

    def mate(r):
        return lax.rem(p_me + r, PLANE)

    def from_mate(r):
        return lax.rem(p_me - r + PLANE, PLANE)

    def layer(d):
        return lax.rem(z - SHIFTS[d] + LAYERS, LAYERS)

    def copy(src, dst, send, recv, device):
        return pltpu.make_async_remote_copy(
            src_ref=src, dst_ref=dst, send_sem=send, recv_sem=recv,
            device_id={"seq": device}, device_id_type=MESH,
        )

    def cross(src, dst, send, recv, device):
        return pltpu.make_async_remote_copy(
            src_ref=src, dst_ref=dst, send_sem=send, recv_sem=recv,
            device_id={"fsdp": device}, device_id_type=MESH,
        )

    next_one, last_one = lax.rem(me + 1, count), lax.rem(me + count - 1, count)
    barrier = pltpu.get_barrier_semaphore()
    for r in range(1, PLANE):
        pl.semaphore_signal(barrier, inc=1, device_id={"seq": z * PLANE + mate(r)}, device_id_type=MESH)
    for s in range(1, LAYERS):
        pl.semaphore_signal(barrier, inc=1, device_id={"seq": col(s)}, device_id_type=MESH)
    pl.semaphore_signal(barrier, inc=1, device_id={"seq": next_one}, device_id_type=MESH)
    pl.semaphore_signal(barrier, inc=1, device_id={"seq": last_one}, device_id_type=MESH)
    for f in range(1, 4):
        pl.semaphore_signal(barrier, inc=1, device_id={"fsdp": lax.rem(row + f, 4)}, device_id_type=MESH)
    pl.semaphore_wait(barrier, 7 + 7 + 2 + 3)

    ways = (1, -1)
    first_hop, second_hop = (front1, back1), (front2, back2)
    own = (k_ref, v_ref)

    def hop1(w, t):
        return copy(own[t], first_hop[w].at[t], hop1_s.at[w, t], hop1_r.at[w, t], col(ways[w]))

    def hop2(w, t):
        return copy(first_hop[w].at[t], second_hop[w].at[t], hop2_s.at[w, t], hop2_r.at[w, t], col(ways[w]))

    def hop3(w, c):
        part = pl.ds(0, 4) if c == 0 else pl.ds(2 * c + 2, 2)
        return copy(pick3.at[w, part], got3.at[w, part], hop3_s.at[w, c], hop3_r.at[w, c], col(ways[w]))

    def hop4(w):
        return copy(got3.at[w, pl.ds(0, 4)], got4.at[w], hop4_s.at[w], hop4_r.at[w], col(ways[w]))

    for t in range(2):
        for w in range(2):
            hop1(w, t).start()

    def halo_copy(side, t):
        block = tokens // BLOCK - 1 if side == 0 else 0
        return copy(
            own[t].at[block], halo.at[side, pl.ds(t * BLOCK, BLOCK)], halo_s.at[side, t], halo_r.at[side, t],
            next_one if side == 0 else last_one,
        )

    for side in range(2):
        for t in range(2):
            halo_copy(side, t).start()

    blocks_here = ids.shape[0]
    lane = lax.broadcasted_iota(jnp.int32, mine_v.shape, 1)
    wanted = jnp.zeros(mine_v.shape, jnp.int32)
    askers = jnp.zeros(mine_v.shape, jnp.int32)
    for b in range(blocks_here):
        for j in range(R):
            hit = lane == lax.div(ids[b, j], blocks_here)
            wanted = jnp.where(hit, lax.rem(ids[b, j], blocks_here), wanted)
            askers = jnp.where(hit, b, askers)
    mine_v[...] = wanted
    inverse_v[...] = askers

    def row_copy(r, at):
        return copy(mine_v, table_v.at[at], t_s.at[r], t_r.at[r], z * PLANE + mate(r))

    def table_copy(w, far):
        k = 2 * w + far - 1
        return copy(table_v, tables_v.at[k], far_s.at[k], far_r.at[k], col(-far * ways[w]))

    for r in range(1, PLANE):
        row_copy(r, p_me).start()
    table_v[p_me] = wanted
    keep_inverse = pltpu.make_async_copy(inverse_v, inverse, local_s.at[0])
    keep_table = pltpu.make_async_copy(table_v, table, local_s.at[1])
    keep_tables = pltpu.make_async_copy(tables_v, tables, local_s.at[2])
    keep_inverse.start()

    piece = G * pair // PLANE
    for g in range(G):
        holder = jnp.full((BLOCK, width), lax.div(shared_ids[g], blocks_here), jnp.int32)
        keep = jnp.where(holder == me, 1.0, 0.0)
        for t in range(2):
            block = own[t][lax.rem(shared_ids[g], blocks_here)].astype(jnp.float32) * keep
            g_mine[pl.ds(g * pair + t * BLOCK, BLOCK), :] = block.astype(jnp.bfloat16)

    def piece_at(p):
        return pl.ds(pl.multiple_of(p * piece, piece), piece)

    def g1(r, p):
        return copy(g_mine.at[piece_at(p)], g_in.at[r], g_s.at[0, r], g_r.at[0, r], z * PLANE + p)

    def g2(s):
        return copy(g_part, g_col.at[s], g_s.at[1, s], g_r.at[1, s], col(s))

    def g3(r, p, at):
        return copy(g_sum, g_all.at[piece_at(at)], g_s.at[2, r], g_r.at[2, r], z * PLANE + p)

    def each(low, high, body):
        def step(i, carry):
            body(i)
            return carry

        lax.fori_loop(low, high, step, 0)

    each(1, PLANE, lambda r: g1(r, mate(r)).start())
    g_in[0] = g_mine[piece_at(p_me), :]

    def choose(d, source):
        owner = layer(d) * PLANE + p_me

        def one(r):
            spot = table[mate(r), 0, owner]
            for t in range(2):
                stage[d, r, pl.ds(t * BLOCK, BLOCK), :] = source(t, spot)

        each(0, PLANE, one)
        fetched[owner] = stage[d, 0]

    def spread_one(d, r, src):
        owner = layer(d) * PLANE + p_me
        return copy(src, fetched.at[owner], in_s.at[d, r], in_r.at[d, r], z * PLANE + mate(r))

    def spread(d):
        each(1, PLANE, lambda r: spread_one(d, r, stage.at[d, r]).start())

    def arrived(d, r):
        owner = layer(d) * PLANE + from_mate(r)
        copy(fetched.at[owner], fetched.at[owner], in_s.at[d, r], in_r.at[d, r], z * PLANE + mate(r)).wait_recv()

    def columns(h):
        return pl.ds(h * HD, HD)

    def attend(owner):
        asker = inverse[0, owner]
        scores = []
        for h in range(heads):
            keys = fetched[owner, pl.ds(0, BLOCK), columns(h)]
            scores.append(lax.dot_general(q_ref[asker, :, columns(h)], keys, NT, preferred_element_type=jnp.float32))
        scores = jnp.concatenate(scores, axis=0) * HD**-0.5
        row_max = jnp.max(scores, axis=1, keepdims=True)
        lifted = jnp.exp(scores - row_max)
        row_sum = jnp.sum(lifted, axis=1, keepdims=True)
        lifted = lifted.astype(jnp.bfloat16)
        parts = [slice(h * BLOCK, (h + 1) * BLOCK) for h in range(heads)]
        for h in range(heads):
            values = fetched[owner, pl.ds(BLOCK, BLOCK), columns(h)]
            far_acc[owner, :, columns(h)] = jnp.dot(lifted[parts[h]], values, preferred_element_type=jnp.float32)
        far_max[owner] = lanes_of([row_max[part] for part in parts])
        far_sum[owner] = lanes_of([row_sum[part] for part in parts])

    def attend_layer(d):
        def one(r):
            @pl.when(r > 0)
            def _():
                arrived(d, r)

            attend(layer(d) * PLANE + from_mate(r))

        each(0, PLANE, one)

    for r in range(1, PLANE):
        row_copy(r, from_mate(r)).wait_recv()
    keep_table.start()
    for w in range(2):
        for far in (1, 2):
            table_copy(w, far).start()
    keep_inverse.wait()
    keep_table.wait()
    choose(0, lambda t, spot: own[t][spot])
    spread(0)

    each(1, PLANE, lambda r: g1(r, mate(r)).wait_recv())
    total = g_in[0]
    for r in range(1, PLANE):
        total = total + g_in[r]
    g_part[...] = total
    each(1, LAYERS, lambda s: g2(s).start())
    g_col[0] = total

    attend_layer(0)

    for t in range(2):
        for w in range(2):
            hop1(w, t).wait_recv()
            hop2(w, t).start()
    for w in range(2):
        choose(1 + w, lambda t, spot: first_hop[w][t, spot])
        spread(1 + w)

    each(1, LAYERS, lambda s: g2(s).wait_recv())
    total = g_col[0]
    for s in range(1, LAYERS):
        total = total + g_col[s]
    g_sum[...] = total
    each(1, PLANE, lambda r: g3(r, mate(r), p_me).start())
    g_all[piece_at(p_me), :] = total

    for side in range(2):
        for t in range(2):
            halo_copy(side, t).wait_recv()
    pads = (key_pad, value_pad)
    for t in range(2):
        pads[t][pl.ds(0, BLOCK), :] = halo[0, pl.ds(t * BLOCK, BLOCK), :]
        pads[t][pl.ds(BLOCK, tokens), :] = own[t][...].reshape(tokens, width)
        pads[t][pl.ds(BLOCK + tokens, BLOCK), :] = halo[1, pl.ds(t * BLOCK, BLOCK), :]
    each(1, PLANE, lambda r: g3(r, mate(r), from_mate(r)).wait_recv())

    tile = 2 * BLOCK
    span = tile + 2 * BLOCK
    steps = tokens // tile

    def near(step):
        wide = span + G * BLOCK
        row_block = lax.broadcasted_iota(jnp.int32, (tile, wide), 0) // BLOCK
        column = lax.broadcasted_iota(jnp.int32, (tile, wide), 1)
        key_block = column // BLOCK
        first = jnp.where((me == 0) & (step == 0), 1, 0)
        last = jnp.where((me == count - 1) & (step == steps - 1), 1, 0)
        listed = (key_block >= row_block) & (key_block <= row_block + 2)
        listed = listed & (key_block >= first) & (key_block < span // BLOCK - last)
        listed = listed | (column >= span)
        rows = pl.ds(pl.multiple_of(step * tile, tile), tile)
        around = pl.ds(pl.multiple_of(step * tile, tile), span)
        maxima, sums = [], []
        for h in range(heads):
            shared = [g_all[pl.ds(b * BLOCK, BLOCK), columns(h)] for b in range(2 * G)]
            keys = jnp.concatenate([key_pad[around, columns(h)]] + shared[0::2], axis=0)
            values = jnp.concatenate([value_pad[around, columns(h)]] + shared[1::2], axis=0)
            query = q_ref[pl.ds(step * (tile // BLOCK), tile // BLOCK), :, columns(h)].reshape(tile, HD)
            scores = lax.dot_general(query, keys, NT, preferred_element_type=jnp.float32)
            scores = jnp.where(listed, scores * HD**-0.5, LOW)
            row_max = jnp.max(scores, axis=1, keepdims=True)
            lifted = jnp.exp(scores - row_max)
            maxima.append(row_max)
            sums.append(jnp.sum(lifted, axis=1, keepdims=True))
            near_acc[rows, columns(h)] = jnp.dot(
                lifted.astype(jnp.bfloat16), values, preferred_element_type=jnp.float32
            )
        near_max[rows, :] = lanes_of(maxima)
        near_sum[rows, :] = lanes_of(sums)

    each(0, steps, near)
    for w in range(2):
        attend_layer(1 + w)

    for w in range(2):
        for far in (1, 2):
            table_copy(w, far).wait_recv()
    keep_tables.start()
    keep_tables.wait()
    for w in range(2):
        for t in range(2):
            hop2(w, t).wait_recv()
        owner = col(-2 * ways[w])

        def one(j, r, far):
            spot = tables[2 * w + far - 1, mate(r), 0, owner]
            for t in range(2):
                pick3[w, j, pl.ds(t * BLOCK, BLOCK), :] = second_hop[w][t, spot]

        each(0, 4, lambda j: one(j, 2 * j + w, 2))
        each(0, PLANE, lambda r: one(4 + r, r, 1))
        for c in range(5):
            hop3(w, c).start()
    for w in range(2):
        choose(3 + w, lambda t, spot: second_hop[w][t, spot])
        spread(3 + w)
    for w in range(2):
        hop3(w, 0).wait_recv()
        hop4(w).start()
    for c in range(1, 5):
        for w in range(2):
            hop3(w, c).wait_recv()
            for r in (2 * c - 2, 2 * c - 1):
                if r == 0:
                    fetched[layer(5 + w) * PLANE + p_me] = got3[w, 4]
                else:
                    spread_one(5 + w, r, got3.at[w, 4 + r]).start()
        if c <= 2:
            attend_layer(2 + c)
    for w in range(2):
        hop4(w).wait_recv()
    for r in range(PLANE):
        if r == 0:
            fetched[layer(7) * PLANE + p_me] = got4[0, 0]
        else:
            spread_one(7, r, got4.at[r % 2, r // 2]).start()
    attend_layer(5)
    attend_layer(6)
    attend_layer(7)

    quarter = tokens // 4

    def merge(block):
        rows = pl.ds(pl.multiple_of(block * BLOCK, BLOCK), BLOCK)
        slots = [lax.div(ids[block, j], blocks_here) for j in range(R)]
        maxima = [near_max[rows, :]] + [far_max[slot] for slot in slots]
        top = maxima[0]
        for one in maxima[1:]:
            top = jnp.maximum(top, one)
        scales = [jnp.exp(one - top) for one in maxima]
        sums = [near_sum[rows, :]] + [far_sum[slot] for slot in slots]
        whole = scales[0] * sums[0]
        for scale, one in zip(scales[1:], sums[1:]):
            whole = whole + scale * one
        scales = [scale / whole for scale in scales]
        for h in range(heads):
            out = scales[0][:, h : h + 1] * near_acc[rows, columns(h)]
            for scale, slot in zip(scales[1:], slots):
                out = out + scale[:, h : h + 1] * far_acc[slot, :, columns(h)]
            context[rows, columns(h)] = out.astype(jnp.bfloat16)

    def quarter_at(f):
        return pl.ds(pl.multiple_of(f * quarter, quarter), quarter)

    def heads_at(f):
        return pl.ds(pl.multiple_of(f * width, width), width)

    blocks = quarter // BLOCK
    for f in (2, 1, 3, 0):
        to = lax.rem(row + f, 4)
        each(0, blocks, lambda b: merge(to * blocks + b))
        if f > 0:
            cross(context.at[quarter_at(to)], heads_ref.at[:, heads_at(row)], c_s.at[f], c_r.at[f], to).start()
        else:
            heads_ref[:, heads_at(row)] = context[quarter_at(row), :]

    for t in range(2):
        for w in range(2):
            hop1(w, t).wait_send()
            hop2(w, t).wait_send()
    for w in range(2):
        for c in range(5):
            hop3(w, c).wait_send()
        hop4(w).wait_send()
    for side in range(2):
        for t in range(2):
            halo_copy(side, t).wait_send()
    for d in range(LAYERS):
        each(1, PLANE, lambda r: spread_one(d, r, fetched.at[0]).wait_send())
    each(1, PLANE, lambda r: g1(r, mate(r)).wait_send())
    each(1, LAYERS, lambda s: g2(s).wait_send())
    each(1, PLANE, lambda r: g3(r, mate(r), p_me).wait_send())
    for r in range(1, PLANE):
        row_copy(r, p_me).wait_send()
    for w in range(2):
        for far in (1, 2):
            table_copy(w, far).wait_send()
    for f in range(1, 4):
        cross(context.at[quarter_at(0)], heads_ref.at[:, heads_at(row)], c_s.at[f], c_r.at[f], row).wait_send()
        came = lax.rem(row - f + 4, 4)
        cross(context.at[quarter_at(0)], heads_ref.at[:, heads_at(came)], c_s.at[f], c_r.at[f], row).wait_recv()


def gather_attend(ids, shared_ids, query, keys, values):
    tokens, width = query.shape[0] * BLOCK, query.shape[2]
    n = PLANE * LAYERS
    pair = 2 * BLOCK
    piece = G * pair // PLANE
    half, full = jnp.bfloat16, jnp.float32
    vmem = pl.BlockSpec(memory_space=pltpu.VMEM)
    smem = pl.BlockSpec(memory_space=pltpu.SMEM)
    sem = pltpu.SemaphoreType.DMA
    hop = pltpu.VMEM((2,) + query.shape, half)
    return pl.pallas_call(
        kernel,
        out_shape=jax.ShapeDtypeStruct((tokens // 4, 4 * width), half),
        in_specs=[smem] * 2 + [vmem] * 3,
        out_specs=vmem,
        scratch_shapes=[
            pltpu.VMEM((n, pair, width), half),
            hop, hop, hop, hop,
            pltpu.VMEM((5, PLANE, pair, width), half),
            pltpu.VMEM((2, 12, pair, width), half),
            pltpu.VMEM((2, 12, pair, width), half),
            pltpu.VMEM((2, 4, pair, width), half),
            pltpu.VMEM((2, pair, width), half),
            pltpu.VMEM((tokens + pair, width), half),
            pltpu.VMEM((tokens + pair, width), half),
            pltpu.VMEM((G * pair, width), half),
            pltpu.VMEM((PLANE, piece, width), half),
            pltpu.VMEM((piece, width), half),
            pltpu.VMEM((LAYERS, piece, width), half),
            pltpu.VMEM((piece, width), half),
            pltpu.VMEM((G * pair, width), half),
            pltpu.VMEM((tokens, width), full),
            pltpu.VMEM((tokens, HD), full),
            pltpu.VMEM((tokens, HD), full),
            pltpu.VMEM((n, BLOCK, width), full),
            pltpu.VMEM((n, BLOCK, HD), full),
            pltpu.VMEM((n, BLOCK, HD), full),
            pltpu.VMEM((tokens, width), half),
            pltpu.VMEM((PLANE, HD), jnp.int32),
            pltpu.VMEM((PLANE, HD), jnp.int32),
            pltpu.VMEM((PLANE, PLANE, HD), jnp.int32),
            pltpu.VMEM((4, PLANE, PLANE, HD), jnp.int32),
            pltpu.SMEM((PLANE, HD), jnp.int32),
            pltpu.SMEM((PLANE, PLANE, HD), jnp.int32),
            pltpu.SMEM((4, PLANE, PLANE, HD), jnp.int32),
            sem((2, 2)), sem((2, 2)), sem((2, 2)), sem((2, 2)),
            sem((2, 5)), sem((2, 5)), sem((2,)), sem((2,)),
            sem((LAYERS, PLANE)), sem((LAYERS, PLANE)),
            sem((2, 2)), sem((2, 2)), sem((3, 8)), sem((3, 8)), sem((4,)), sem((4,)),
            sem((PLANE,)), sem((PLANE,)), sem((4,)), sem((4,)), sem((3,)),
        ],
        compiler_params=pltpu.CompilerParams(
            collective_id=0, has_side_effects=True, vmem_limit_bytes=58 << 20
        ),
        cost_estimate=pl.CostEstimate(flops=3 * 10**9, bytes_accessed=10 * 10**6, transcendentals=4 * 10**6),
    )(ids, shared_ids, query, keys, values)


def on_device(query_rows, key_rows, value_rows, out_weight, random_ids, global_ids):
    tokens, width = query_rows.shape
    blocks = tokens // BLOCK
    weight = lax.all_gather(out_weight, "fsdp", axis=0, tiled=True)
    rows = [array.reshape(blocks, BLOCK, width) for array in (query_rows, key_rows, value_rows)]
    all_heads = gather_attend(random_ids, global_ids, *rows)
    return jnp.dot(all_heads, weight, preferred_element_type=jnp.float32).astype(jnp.bfloat16)


def solution(mesh):
    return jax.shard_map(
        on_device,
        mesh=mesh,
        in_specs=(
            P("seq", "fsdp"),
            P("seq", "fsdp"),
            P("seq", "fsdp"),
            P("fsdp", None),
            P("seq", None),
            P(),
        ),
        out_specs=P(("seq", "fsdp"), None),
        check_vma=False,
    )
```

```python
import jax
import jax.numpy as jnp
from jax import lax
from jax.experimental import pallas as pl
from jax.experimental.pallas import tpu as pltpu
from jax.sharding import PartitionSpec as P

HD = 128
BLOCK = 64
G = 2
R = 3
LOW = -1e30
NT = (((1,), (1,)), ((), ()))
MESH = pl.DeviceIdType.MESH
PLANE = 8
LAYERS = 8
SHIFTS = (0, 1, -1, 2, -2, 3, -3, 4)


def lanes_of(parts):
    rows = parts[0].shape[0]
    lane = lax.broadcasted_iota(jnp.int32, (rows, HD), 1)
    out = jnp.zeros((rows, HD), jnp.float32)
    for i, part in enumerate(parts):
        out = jnp.where(lane == i, part, out)
    return out


def kernel(
    ids, shared_ids,
    q_ref, k_ref, v_ref, w_ref,
    heads_ref, weight_ref,
    fetched,
    front1_k, front1_v, back1_k, back1_v, front2_k, front2_v, back2_k, back2_v, stage, pick3, got3, got4,
    halo, key_pad, value_pad, g_mine, g_in, g_part, g_col, g_sum, g_all,
    near_acc, near_max, near_sum, far_acc, far_max, far_sum, context,
    mine_v, inverse_v, table_v, tables_v, inverse, table, tables,
    hop1_s, hop1_r, hop2_s, hop2_r, hop3_s, hop3_r, hop4_s, hop4_r,
    in_s, in_r, halo_s, halo_r, g_s, g_r, c_s, c_r, t_s, t_r, far_s, far_r, local_s,
    row_s, row_r, core_s, core_r,
):
    me = lax.axis_index("seq")
    row = lax.axis_index("fsdp")
    z, p_me = me // PLANE, me % PLANE
    count = PLANE * LAYERS
    tokens, width = key_pad.shape[0] - 2 * BLOCK, q_ref.shape[2]
    heads = width // HD
    pair = 2 * BLOCK

    def col(shift):
        return lax.rem(z + shift + LAYERS, LAYERS) * PLANE + p_me

    def mate(r):
        return lax.rem(p_me + r, PLANE)

    def from_mate(r):
        return lax.rem(p_me - r + PLANE, PLANE)

    def layer(d):
        return lax.rem(z - SHIFTS[d] + LAYERS, LAYERS)

    def copy(src, dst, send, recv, device):
        return pltpu.make_async_remote_copy(
            src_ref=src, dst_ref=dst, send_sem=send, recv_sem=recv,
            device_id={"seq": device}, device_id_type=MESH,
        )

    def cross(src, dst, send, recv, device):
        return pltpu.make_async_remote_copy(
            src_ref=src, dst_ref=dst, send_sem=send, recv_sem=recv,
            device_id={"fsdp": device}, device_id_type=MESH,
        )

    next_one, last_one = lax.rem(me + 1, count), lax.rem(me + count - 1, count)
    barrier = pltpu.get_barrier_semaphore()
    for r in range(1, PLANE):
        pl.semaphore_signal(barrier, inc=1, device_id={"seq": z * PLANE + mate(r)}, device_id_type=MESH)
    for s in range(1, LAYERS):
        pl.semaphore_signal(barrier, inc=1, device_id={"seq": col(s)}, device_id_type=MESH)
    pl.semaphore_signal(barrier, inc=1, device_id={"seq": next_one}, device_id_type=MESH)
    pl.semaphore_signal(barrier, inc=1, device_id={"seq": last_one}, device_id_type=MESH)
    for f in range(1, 4):
        pl.semaphore_signal(barrier, inc=1, device_id={"fsdp": lax.rem(row + f, 4)}, device_id_type=MESH)
    pl.semaphore_wait(barrier, 7 + 7 + 2 + 3)

    ways = (1, -1)
    first_hop = ((front1_k, front1_v), (back1_k, back1_v))
    second_hop = ((front2_k, front2_v), (back2_k, back2_v))
    own = (k_ref, v_ref)

    def hop1(w, t):
        return copy(own[t], first_hop[w][t], hop1_s.at[w, t], hop1_r.at[w, t], col(ways[w]))

    def hop2(w, t):
        return copy(first_hop[w][t], second_hop[w][t], hop2_s.at[w, t], hop2_r.at[w, t], col(ways[w]))

    def hop3(w, t, c):
        part = pl.ds(4 * c, 4)
        return copy(
            pick3.at[w, t, part], got3.at[w, t, part], hop3_s.at[w, t, c], hop3_r.at[w, t, c], col(ways[w])
        )

    def hop4(w, t):
        return copy(got3.at[w, t, pl.ds(0, 4)], got4.at[w, t], hop4_s.at[w, t], hop4_r.at[w, t], col(ways[w]))

    core = lax.rem(me, 2)
    depth = w_ref.shape[0]
    part_rows = pl.ds(pl.multiple_of(core * (depth // 2), depth // 2), depth // 2)

    def row_weight(f, at):
        return cross(
            w_ref.at[part_rows], weight_ref.at[at, part_rows], row_s.at[f], row_r.at[f], lax.rem(row + f, 4)
        )

    def core_weight(f, rows):
        came = lax.rem(row - f + 4, 4)
        return copy(
            weight_ref.at[came, rows], weight_ref.at[came, rows], core_s.at[f], core_r.at[f], me + 1 - 2 * core
        )

    own_weight = pltpu.make_async_copy(w_ref, weight_ref.at[row], local_s.at[3])

    for t in range(2):
        for w in range(2):
            hop1(w, t).start()
    for f in (1, 3, 2):
        row_weight(f, row).start()
    own_weight.start()

    def halo_copy(side, t):
        block = tokens // BLOCK - 1 if side == 0 else 0
        return copy(
            own[t].at[block], halo.at[side, pl.ds(t * BLOCK, BLOCK)], halo_s.at[side, t], halo_r.at[side, t],
            next_one if side == 0 else last_one,
        )

    for side in range(2):
        for t in range(2):
            halo_copy(side, t).start()

    blocks_here = ids.shape[0]
    lane = lax.broadcasted_iota(jnp.int32, mine_v.shape, 1)
    wanted = jnp.zeros(mine_v.shape, jnp.int32)
    askers = jnp.zeros(mine_v.shape, jnp.int32)
    for b in range(blocks_here):
        for j in range(R):
            hit = lane == lax.div(ids[b, j], blocks_here)
            wanted = jnp.where(hit, lax.rem(ids[b, j], blocks_here), wanted)
            askers = jnp.where(hit, b, askers)
    mine_v[...] = wanted
    inverse_v[...] = askers

    def row_copy(r, at):
        return copy(mine_v, table_v.at[at], t_s.at[r], t_r.at[r], z * PLANE + mate(r))

    def table_copy(w, far):
        k = 2 * w + far - 1
        return copy(table_v, tables_v.at[k], far_s.at[k], far_r.at[k], col(-far * ways[w]))

    for r in range(1, PLANE):
        row_copy(r, p_me).start()
    table_v[p_me] = wanted
    keep_inverse = pltpu.make_async_copy(inverse_v, inverse, local_s.at[0])
    keep_table = pltpu.make_async_copy(table_v, table, local_s.at[1])
    keep_tables = pltpu.make_async_copy(tables_v, tables, local_s.at[2])
    keep_inverse.start()

    piece = G * pair // PLANE
    for g in range(G):
        holder = jnp.full((BLOCK, width), lax.div(shared_ids[g], blocks_here), jnp.int32)
        keep = jnp.where(holder == me, 1.0, 0.0)
        for t in range(2):
            block = own[t][lax.rem(shared_ids[g], blocks_here)].astype(jnp.float32) * keep
            g_mine[pl.ds(g * pair + t * BLOCK, BLOCK), :] = block.astype(jnp.bfloat16)

    def piece_at(p):
        return pl.ds(pl.multiple_of(p * piece, piece), piece)

    def g1(r, p):
        return copy(g_mine.at[piece_at(p)], g_in.at[r], g_s.at[0, r], g_r.at[0, r], z * PLANE + p)

    def g2(s):
        return copy(g_part, g_col.at[s], g_s.at[1, s], g_r.at[1, s], col(s))

    def g3(r, p, at):
        return copy(g_sum, g_all.at[piece_at(at)], g_s.at[2, r], g_r.at[2, r], z * PLANE + p)

    def each(low, high, body):
        def step(i, carry):
            body(i)
            return carry

        lax.fori_loop(low, high, step, 0)

    each(1, PLANE, lambda r: g1(r, mate(r)).start())
    g_in[0] = g_mine[piece_at(p_me), :]

    def choose(d, t, read):
        owner = layer(d) * PLANE + p_me

        def one(r):
            stage[d, t, r] = read(table[mate(r), 0, owner])

        each(0, PLANE, one)
        fetched[t, owner] = stage[d, t, 0]

    def spread_one(d, t, r, src):
        owner = layer(d) * PLANE + p_me
        return copy(src, fetched.at[t, owner], in_s.at[t, d, r], in_r.at[t, d, r], z * PLANE + mate(r))

    def spread(d, t):
        each(1, PLANE, lambda r: spread_one(d, t, r, stage.at[d, t, r]).start())

    def arrived(d, r):
        owner = layer(d) * PLANE + from_mate(r)
        for t in range(2):
            spot = fetched.at[t, owner]
            copy(spot, spot, in_s.at[t, d, r], in_r.at[t, d, r], z * PLANE + mate(r)).wait_recv()

    def columns(h):
        return pl.ds(h * HD, HD)

    def attend(owner):
        asker = inverse[0, owner]
        scores = []
        for h in range(heads):
            keys = fetched[0, owner, :, columns(h)]
            scores.append(lax.dot_general(q_ref[asker, :, columns(h)], keys, NT, preferred_element_type=jnp.float32))
        scores = jnp.concatenate(scores, axis=0) * HD**-0.5
        row_max = jnp.max(scores, axis=1, keepdims=True)
        lifted = jnp.exp(scores - row_max)
        row_sum = jnp.sum(lifted, axis=1, keepdims=True)
        lifted = lifted.astype(jnp.bfloat16)
        parts = [slice(h * BLOCK, (h + 1) * BLOCK) for h in range(heads)]
        for h in range(heads):
            values = fetched[1, owner, :, columns(h)]
            far_acc[owner, :, columns(h)] = jnp.dot(lifted[parts[h]], values, preferred_element_type=jnp.float32)
        far_max[owner] = lanes_of([row_max[part] for part in parts])
        far_sum[owner] = lanes_of([row_sum[part] for part in parts])

    def attend_layer(d):
        def one(r):
            @pl.when(r > 0)
            def _():
                arrived(d, r)

            attend(layer(d) * PLANE + from_mate(r))

        each(0, PLANE, one)

    for r in range(1, PLANE):
        row_copy(r, from_mate(r)).wait_recv()
    keep_table.start()
    for w in range(2):
        for far in (1, 2):
            table_copy(w, far).start()
    keep_inverse.wait()
    keep_table.wait()
    for t in range(2):
        choose(0, t, lambda spot: own[t][spot])
        spread(0, t)

    each(1, PLANE, lambda r: g1(r, mate(r)).wait_recv())
    total = g_in[0]
    for r in range(1, PLANE):
        total = total + g_in[r]
    g_part[...] = total
    each(1, LAYERS, lambda s: g2(s).start())
    g_col[0] = total

    attend_layer(0)

    for t in range(2):
        for w in range(2):
            hop1(w, t).wait_recv()
            hop2(w, t).start()
        for w in range(2):
            choose(1 + w, t, lambda spot: first_hop[w][t][spot])
            spread(1 + w, t)

    each(1, LAYERS, lambda s: g2(s).wait_recv())
    total = g_col[0]
    for s in range(1, LAYERS):
        total = total + g_col[s]
    g_sum[...] = total
    each(1, PLANE, lambda r: g3(r, mate(r), p_me).start())
    g_all[piece_at(p_me), :] = total

    for side in range(2):
        for t in range(2):
            halo_copy(side, t).wait_recv()
    pads = (key_pad, value_pad)
    for t in range(2):
        pads[t][pl.ds(0, BLOCK), :] = halo[0, pl.ds(t * BLOCK, BLOCK), :]
        pads[t][pl.ds(BLOCK, tokens), :] = own[t][...].reshape(tokens, width)
        pads[t][pl.ds(BLOCK + tokens, BLOCK), :] = halo[1, pl.ds(t * BLOCK, BLOCK), :]
    each(1, PLANE, lambda r: g3(r, mate(r), from_mate(r)).wait_recv())

    tile = 2 * BLOCK
    span = tile + 2 * BLOCK
    steps = tokens // tile

    def near(step):
        wide = span + G * BLOCK
        row_block = lax.broadcasted_iota(jnp.int32, (tile, wide), 0) // BLOCK
        column = lax.broadcasted_iota(jnp.int32, (tile, wide), 1)
        key_block = column // BLOCK
        first = jnp.where((me == 0) & (step == 0), 1, 0)
        last = jnp.where((me == count - 1) & (step == steps - 1), 1, 0)
        listed = (key_block >= row_block) & (key_block <= row_block + 2)
        listed = listed & (key_block >= first) & (key_block < span // BLOCK - last)
        listed = listed | (column >= span)
        rows = pl.ds(pl.multiple_of(step * tile, tile), tile)
        around = pl.ds(pl.multiple_of(step * tile, tile), span)
        maxima, sums = [], []
        for h in range(heads):
            shared = [g_all[pl.ds(b * BLOCK, BLOCK), columns(h)] for b in range(2 * G)]
            keys = jnp.concatenate([key_pad[around, columns(h)]] + shared[0::2], axis=0)
            values = jnp.concatenate([value_pad[around, columns(h)]] + shared[1::2], axis=0)
            query = q_ref[pl.ds(step * (tile // BLOCK), tile // BLOCK), :, columns(h)].reshape(tile, HD)
            scores = lax.dot_general(query, keys, NT, preferred_element_type=jnp.float32)
            scores = jnp.where(listed, scores * HD**-0.5, LOW)
            row_max = jnp.max(scores, axis=1, keepdims=True)
            lifted = jnp.exp(scores - row_max)
            maxima.append(row_max)
            sums.append(jnp.sum(lifted, axis=1, keepdims=True))
            near_acc[rows, columns(h)] = jnp.dot(
                lifted.astype(jnp.bfloat16), values, preferred_element_type=jnp.float32
            )
        near_max[rows, :] = lanes_of(maxima)
        near_sum[rows, :] = lanes_of(sums)

    each(0, steps, near)
    for w in range(2):
        attend_layer(1 + w)

    for w in range(2):
        for far in (1, 2):
            table_copy(w, far).wait_recv()
    keep_tables.start()
    keep_tables.wait()
    for t in range(2):
        for w in range(2):
            hop2(w, t).wait_recv()
            owner = col(-2 * ways[w])

            def one(j, r, far):
                pick3[w, t, j] = second_hop[w][t][tables[2 * w + far - 1, mate(r), 0, owner]]

            each(0, 4, lambda j: one(j, 2 * j + w, 2))
            hop3(w, t, 0).start()
            each(0, PLANE, lambda r: one(4 + r, r, 1))
            for c in (1, 2):
                hop3(w, t, c).start()
        for w in range(2):
            choose(3 + w, t, lambda spot: second_hop[w][t][spot])
            spread(3 + w, t)
    for t in range(2):
        for w in range(2):
            hop3(w, t, 0).wait_recv()
            hop4(w, t).start()
        for c in (1, 2):
            for w in range(2):
                hop3(w, t, c).wait_recv()
                for r in range(4 * c - 4, 4 * c):
                    if r == 0:
                        fetched[t, layer(5 + w) * PLANE + p_me] = got3[w, t, 4]
                    else:
                        spread_one(5 + w, t, r, got3.at[w, t, 4 + r]).start()
        if t == 0:
            for f in (1, 3, 2):
                row_weight(f, lax.rem(row - f + 4, 4)).wait_recv()
                core_weight(f, part_rows).start()
            for w in range(2):
                attend_layer(3 + w)
    for t in range(2):
        for w in range(2):
            hop4(w, t).wait_recv()
            for j in range(4):
                r = 2 * j + w
                if r == 0:
                    fetched[t, layer(7) * PLANE + p_me] = got4[w, t, j]
                else:
                    spread_one(7, t, r, got4.at[w, t, j]).start()
    attend_layer(5)
    attend_layer(6)
    attend_layer(7)

    quarter = tokens // 4

    def merge(block):
        rows = pl.ds(pl.multiple_of(block * BLOCK, BLOCK), BLOCK)
        slots = [lax.div(ids[block, j], blocks_here) for j in range(R)]
        maxima = [near_max[rows, :]] + [far_max[slot] for slot in slots]
        top = maxima[0]
        for one in maxima[1:]:
            top = jnp.maximum(top, one)
        scales = [jnp.exp(one - top) for one in maxima]
        sums = [near_sum[rows, :]] + [far_sum[slot] for slot in slots]
        whole = scales[0] * sums[0]
        for scale, one in zip(scales[1:], sums[1:]):
            whole = whole + scale * one
        scales = [scale / whole for scale in scales]
        for h in range(heads):
            out = scales[0][:, h : h + 1] * near_acc[rows, columns(h)]
            for scale, slot in zip(scales[1:], slots):
                out = out + scale[:, h : h + 1] * far_acc[slot, :, columns(h)]
            context[rows, columns(h)] = out.astype(jnp.bfloat16)

    def quarter_at(f):
        return pl.ds(pl.multiple_of(f * quarter, quarter), quarter)

    def heads_at(f):
        return pl.ds(pl.multiple_of(f * width, width), width)

    blocks = quarter // BLOCK
    for f in (2, 1, 3, 0):
        to = lax.rem(row + f, 4)
        each(0, blocks, lambda b: merge(to * blocks + b))
        if f > 0:
            cross(context.at[quarter_at(to)], heads_ref.at[:, heads_at(row)], c_s.at[f], c_r.at[f], to).start()
        else:
            heads_ref[:, heads_at(row)] = context[quarter_at(row), :]

    for t in range(2):
        for w in range(2):
            hop1(w, t).wait_send()
            hop2(w, t).wait_send()
            for c in range(3):
                hop3(w, t, c).wait_send()
            hop4(w, t).wait_send()
    for side in range(2):
        for t in range(2):
            halo_copy(side, t).wait_send()
    for d in range(LAYERS):
        for t in range(2):
            each(1, PLANE, lambda r: spread_one(d, t, r, fetched.at[t, 0]).wait_send())
    each(1, PLANE, lambda r: g1(r, mate(r)).wait_send())
    each(1, LAYERS, lambda s: g2(s).wait_send())
    each(1, PLANE, lambda r: g3(r, mate(r), p_me).wait_send())
    for r in range(1, PLANE):
        row_copy(r, p_me).wait_send()
    for w in range(2):
        for far in (1, 2):
            table_copy(w, far).wait_send()
    own_weight.wait()
    other_rows = pl.ds(pl.multiple_of((1 - core) * (depth // 2), depth // 2), depth // 2)
    for f in range(1, 4):
        row_weight(f, row).wait_send()
        core_weight(f, part_rows).wait_send()
        core_weight(f, other_rows).wait_recv()
    for f in range(1, 4):
        cross(context.at[quarter_at(0)], heads_ref.at[:, heads_at(row)], c_s.at[f], c_r.at[f], row).wait_send()
        came = lax.rem(row - f + 4, 4)
        cross(context.at[quarter_at(0)], heads_ref.at[:, heads_at(came)], c_s.at[f], c_r.at[f], row).wait_recv()


def gather_attend(ids, shared_ids, query, keys, values, weight):
    tokens, width = query.shape[0] * BLOCK, query.shape[2]
    n = PLANE * LAYERS
    pair = 2 * BLOCK
    piece = G * pair // PLANE
    half, full = jnp.bfloat16, jnp.float32
    vmem = pl.BlockSpec(memory_space=pltpu.VMEM)
    smem = pl.BlockSpec(memory_space=pltpu.SMEM)
    sem = pltpu.SemaphoreType.DMA
    hop = pltpu.VMEM(query.shape, half)
    return pl.pallas_call(
        kernel,
        out_shape=[
            jax.ShapeDtypeStruct((tokens // 4, 4 * width), half),
            jax.ShapeDtypeStruct((4,) + weight.shape, half),
        ],
        in_specs=[smem] * 2 + [vmem] * 3 + [pl.BlockSpec(memory_space=pl.ANY)],
        out_specs=[vmem, pl.BlockSpec(memory_space=pl.ANY)],
        scratch_shapes=[
            pltpu.VMEM((2, n, BLOCK, width), half),
            hop, hop, hop, hop, hop, hop, hop, hop,
            pltpu.VMEM((5, 2, PLANE, BLOCK, width), half),
            pltpu.VMEM((2, 2, 12, BLOCK, width), half),
            pltpu.VMEM((2, 2, 12, BLOCK, width), half),
            pltpu.VMEM((2, 2, 4, BLOCK, width), half),
            pltpu.VMEM((2, pair, width), half),
            pltpu.VMEM((tokens + pair, width), half),
            pltpu.VMEM((tokens + pair, width), half),
            pltpu.VMEM((G * pair, width), half),
            pltpu.VMEM((PLANE, piece, width), half),
            pltpu.VMEM((piece, width), half),
            pltpu.VMEM((LAYERS, piece, width), half),
            pltpu.VMEM((piece, width), half),
            pltpu.VMEM((G * pair, width), half),
            pltpu.VMEM((tokens, width), full),
            pltpu.VMEM((tokens, HD), full),
            pltpu.VMEM((tokens, HD), full),
            pltpu.VMEM((n, BLOCK, width), full),
            pltpu.VMEM((n, BLOCK, HD), full),
            pltpu.VMEM((n, BLOCK, HD), full),
            pltpu.VMEM((tokens, width), half),
            pltpu.VMEM((PLANE, HD), jnp.int32),
            pltpu.VMEM((PLANE, HD), jnp.int32),
            pltpu.VMEM((PLANE, PLANE, HD), jnp.int32),
            pltpu.VMEM((4, PLANE, PLANE, HD), jnp.int32),
            pltpu.SMEM((PLANE, HD), jnp.int32),
            pltpu.SMEM((PLANE, PLANE, HD), jnp.int32),
            pltpu.SMEM((4, PLANE, PLANE, HD), jnp.int32),
            sem((2, 2)), sem((2, 2)), sem((2, 2)), sem((2, 2)),
            sem((2, 2, 3)), sem((2, 2, 3)), sem((2, 2)), sem((2, 2)),
            sem((2, LAYERS, PLANE)), sem((2, LAYERS, PLANE)),
            sem((2, 2)), sem((2, 2)), sem((3, 8)), sem((3, 8)), sem((4,)), sem((4,)),
            sem((PLANE,)), sem((PLANE,)), sem((4,)), sem((4,)), sem((4,)),
            sem((4,)), sem((4,)), sem((4,)), sem((4,)),
        ],
        compiler_params=pltpu.CompilerParams(
            collective_id=0, has_side_effects=True, vmem_limit_bytes=58 << 20
        ),
        cost_estimate=pl.CostEstimate(flops=3 * 10**9, bytes_accessed=10 * 10**6, transcendentals=4 * 10**6),
    )(ids, shared_ids, query, keys, values, weight)


def on_device(query_rows, key_rows, value_rows, out_weight, random_ids, global_ids):
    tokens, width = query_rows.shape
    blocks = tokens // BLOCK
    rows = [array.reshape(blocks, BLOCK, width) for array in (query_rows, key_rows, value_rows)]
    all_heads, weight = gather_attend(random_ids, global_ids, *rows, out_weight)
    weight = weight.reshape(-1, out_weight.shape[1])
    return jnp.dot(all_heads, weight, preferred_element_type=jnp.float32).astype(jnp.bfloat16)


def solution(mesh):
    return jax.shard_map(
        on_device,
        mesh=mesh,
        in_specs=(
            P("seq", "fsdp"),
            P("seq", "fsdp"),
            P("seq", "fsdp"),
            P("fsdp", None),
            P("seq", None),
            P(),
        ),
        out_specs=P(("seq", "fsdp"), None),
        check_vma=False,
    )
```

```python
import jax
import jax.numpy as jnp
from jax import lax
from jax.experimental import pallas as pl
from jax.experimental.pallas import tpu as pltpu
from jax.sharding import PartitionSpec as P

HD = 128
BLOCK = 64
G = 2
R = 3
LOW = -1e30
NT = (((1,), (1,)), ((), ()))
MESH = pl.DeviceIdType.MESH
PLANE = 8
LAYERS = 8
SHIFTS = (0, 1, -1, 2, -2, 3, -3, 4)


def lanes_of(parts):
    rows = parts[0].shape[0]
    lane = lax.broadcasted_iota(jnp.int32, (rows, HD), 1)
    out = jnp.zeros((rows, HD), jnp.float32)
    for i, part in enumerate(parts):
        out = jnp.where(lane == i, part, out)
    return out


def kernel(
    ids, shared_ids,
    q_ref, k_ref, v_ref, w_ref,
    heads_ref, weight_ref,
    fetched,
    front1_k, front1_v, back1_k, back1_v, front2_k, front2_v, back2_k, back2_v, stage, pick3, got3, got4,
    halo, key_pad, value_pad, g_mine, g_in, g_part, g_col, g_sum, g_all,
    near_acc, near_max, near_sum, far_acc, far_max, far_sum, context,
    mine_v, inverse_v, table_v, tables_v, inverse, table, tables,
    hop1_s, hop1_r, hop2_s, hop2_r, hop3_s, hop3_r, hop4_s, hop4_r, relay_s, relay_r,
    in_s, in_r, halo_s, halo_r, g_s, g_r, c_s, c_r, t_s, t_r, far_s, far_r, local_s,
    row_s, row_r, core_s, core_r,
):
    me = lax.axis_index("seq")
    row = lax.axis_index("fsdp")
    z, p_me = me // PLANE, me % PLANE
    count = PLANE * LAYERS
    tokens, width = key_pad.shape[0] - 2 * BLOCK, q_ref.shape[2]
    heads = width // HD
    pair = 2 * BLOCK

    def col(shift):
        return lax.rem(z + shift + LAYERS, LAYERS) * PLANE + p_me

    def mate(r):
        return lax.rem(p_me + r, PLANE)

    def from_mate(r):
        return lax.rem(p_me - r + PLANE, PLANE)

    def layer(d):
        return lax.rem(z - SHIFTS[d] + LAYERS, LAYERS)

    def copy(src, dst, send, recv, device):
        return pltpu.make_async_remote_copy(
            src_ref=src, dst_ref=dst, send_sem=send, recv_sem=recv,
            device_id={"seq": device}, device_id_type=MESH,
        )

    def cross(src, dst, send, recv, device):
        return pltpu.make_async_remote_copy(
            src_ref=src, dst_ref=dst, send_sem=send, recv_sem=recv,
            device_id={"fsdp": device}, device_id_type=MESH,
        )

    next_one, last_one = lax.rem(me + 1, count), lax.rem(me + count - 1, count)
    barrier = pltpu.get_barrier_semaphore()
    for r in range(1, PLANE):
        pl.semaphore_signal(barrier, inc=1, device_id={"seq": z * PLANE + mate(r)}, device_id_type=MESH)
    for s in range(1, LAYERS):
        pl.semaphore_signal(barrier, inc=1, device_id={"seq": col(s)}, device_id_type=MESH)
    pl.semaphore_signal(barrier, inc=1, device_id={"seq": next_one}, device_id_type=MESH)
    pl.semaphore_signal(barrier, inc=1, device_id={"seq": last_one}, device_id_type=MESH)
    for f in range(1, 4):
        pl.semaphore_signal(barrier, inc=1, device_id={"fsdp": lax.rem(row + f, 4)}, device_id_type=MESH)
    pl.semaphore_wait(barrier, 7 + 7 + 2 + 3)

    ways = (1, -1)
    first_hop = ((front1_k, front1_v), (back1_k, back1_v))
    second_hop = ((front2_k, front2_v), (back2_k, back2_v))
    own = (k_ref, v_ref)

    def hop1(w, t):
        return copy(own[t], first_hop[w][t], hop1_s.at[w, t], hop1_r.at[w, t], col(ways[w]))

    def hop2(w, t):
        return copy(first_hop[w][t], second_hop[w][t], hop2_s.at[w, t], hop2_r.at[w, t], col(ways[w]))

    def hop3(w, t, c):
        part = pl.ds(4 * c, 4)
        return copy(
            pick3.at[w, t, part], got3.at[w, t, part], hop3_s.at[w, t, c], hop3_r.at[w, t, c], col(ways[w])
        )

    def relay(w, t, j):
        return copy(
            got3.at[w, t, j], got4.at[w, t, j], relay_s.at[w, t, j], relay_r.at[w, t, j],
            z * PLANE + mate(2 * j + w),
        )

    def hop4(w, t, j):
        src = got3.at[w, t, j] if 2 * j + w == 0 else got4.at[w, t, j]
        owner = col(-3 * ways[w]) - p_me + from_mate(2 * j + w)
        return copy(src, fetched.at[t, owner], hop4_s.at[w, t, j], hop4_r.at[w, t, j], col(ways[w]))

    def last_arrived(w, t, j):
        spot = fetched.at[t, layer(7) * PLANE + from_mate(2 * j + w)]
        copy(spot, spot, hop4_s.at[w, t, j], hop4_r.at[w, t, j], col(ways[w])).wait_recv()

    core = lax.rem(me, 2)
    depth = w_ref.shape[0]
    part_rows = pl.ds(pl.multiple_of(core * (depth // 2), depth // 2), depth // 2)

    def row_weight(f, at):
        return cross(
            w_ref.at[part_rows], weight_ref.at[at, part_rows], row_s.at[f], row_r.at[f], lax.rem(row + f, 4)
        )

    def core_weight(f, rows):
        came = lax.rem(row - f + 4, 4)
        return copy(
            weight_ref.at[came, rows], weight_ref.at[came, rows], core_s.at[f], core_r.at[f], me + 1 - 2 * core
        )

    own_weight = pltpu.make_async_copy(w_ref, weight_ref.at[row], local_s.at[3])

    for t in range(2):
        for w in range(2):
            hop1(w, t).start()
    for f in (1, 3, 2):
        row_weight(f, row).start()
    own_weight.start()

    def halo_copy(side, t):
        block = tokens // BLOCK - 1 if side == 0 else 0
        return copy(
            own[t].at[block], halo.at[side, pl.ds(t * BLOCK, BLOCK)], halo_s.at[side, t], halo_r.at[side, t],
            next_one if side == 0 else last_one,
        )

    for side in range(2):
        for t in range(2):
            halo_copy(side, t).start()

    blocks_here = ids.shape[0]
    lane = lax.broadcasted_iota(jnp.int32, mine_v.shape, 1)
    wanted = jnp.zeros(mine_v.shape, jnp.int32)
    askers = jnp.zeros(mine_v.shape, jnp.int32)
    for b in range(blocks_here):
        for j in range(R):
            hit = lane == lax.div(ids[b, j], blocks_here)
            wanted = jnp.where(hit, lax.rem(ids[b, j], blocks_here), wanted)
            askers = jnp.where(hit, b, askers)
    mine_v[...] = wanted
    inverse_v[...] = askers

    def row_copy(r, at):
        return copy(mine_v, table_v.at[at], t_s.at[r], t_r.at[r], z * PLANE + mate(r))

    def table_copy(w, far):
        k = 2 * w + far - 1
        return copy(table_v, tables_v.at[k], far_s.at[k], far_r.at[k], col(-far * ways[w]))

    for r in range(1, PLANE):
        row_copy(r, p_me).start()
    table_v[p_me] = wanted
    keep_inverse = pltpu.make_async_copy(inverse_v, inverse, local_s.at[0])
    keep_table = pltpu.make_async_copy(table_v, table, local_s.at[1])
    keep_tables = pltpu.make_async_copy(tables_v, tables, local_s.at[2])
    keep_inverse.start()

    piece = G * pair // PLANE
    for g in range(G):
        holder = jnp.full((BLOCK, width), lax.div(shared_ids[g], blocks_here), jnp.int32)
        keep = jnp.where(holder == me, 1.0, 0.0)
        for t in range(2):
            block = own[t][lax.rem(shared_ids[g], blocks_here)].astype(jnp.float32) * keep
            g_mine[pl.ds(g * pair + t * BLOCK, BLOCK), :] = block.astype(jnp.bfloat16)

    def piece_at(p):
        return pl.ds(pl.multiple_of(p * piece, piece), piece)

    def g1(r, p):
        return copy(g_mine.at[piece_at(p)], g_in.at[r], g_s.at[0, r], g_r.at[0, r], z * PLANE + p)

    def g2(s):
        return copy(g_part, g_col.at[s], g_s.at[1, s], g_r.at[1, s], col(s))

    def g3(r, p, at):
        return copy(g_sum, g_all.at[piece_at(at)], g_s.at[2, r], g_r.at[2, r], z * PLANE + p)

    def each(low, high, body):
        def step(i, carry):
            body(i)
            return carry

        lax.fori_loop(low, high, step, 0)

    each(1, PLANE, lambda r: g1(r, mate(r)).start())
    g_in[0] = g_mine[piece_at(p_me), :]

    def choose(d, t, read):
        owner = layer(d) * PLANE + p_me

        def one(r):
            stage[d, t, r] = read(table[mate(r), 0, owner])

        each(0, PLANE, one)
        fetched[t, owner] = stage[d, t, 0]

    def spread_one(d, t, r, src):
        owner = layer(d) * PLANE + p_me
        return copy(src, fetched.at[t, owner], in_s.at[t, d, r], in_r.at[t, d, r], z * PLANE + mate(r))

    def spread(d, t):
        each(1, PLANE, lambda r: spread_one(d, t, r, stage.at[d, t, r]).start())

    def arrived(d, r):
        owner = layer(d) * PLANE + from_mate(r)
        for t in range(2):
            spot = fetched.at[t, owner]
            copy(spot, spot, in_s.at[t, d, r], in_r.at[t, d, r], z * PLANE + mate(r)).wait_recv()

    def columns(h):
        return pl.ds(h * HD, HD)

    def attend(owner):
        asker = inverse[0, owner]
        scores = []
        for h in range(heads):
            keys = fetched[0, owner, :, columns(h)]
            scores.append(lax.dot_general(q_ref[asker, :, columns(h)], keys, NT, preferred_element_type=jnp.float32))
        scores = jnp.concatenate(scores, axis=0) * HD**-0.5
        row_max = jnp.max(scores, axis=1, keepdims=True)
        lifted = jnp.exp(scores - row_max)
        row_sum = jnp.sum(lifted, axis=1, keepdims=True)
        lifted = lifted.astype(jnp.bfloat16)
        parts = [slice(h * BLOCK, (h + 1) * BLOCK) for h in range(heads)]
        for h in range(heads):
            values = fetched[1, owner, :, columns(h)]
            far_acc[owner, :, columns(h)] = jnp.dot(lifted[parts[h]], values, preferred_element_type=jnp.float32)
        far_max[owner] = lanes_of([row_max[part] for part in parts])
        far_sum[owner] = lanes_of([row_sum[part] for part in parts])

    def attend_layer(d):
        def one(r):
            @pl.when(r > 0)
            def _():
                arrived(d, r)

            attend(layer(d) * PLANE + from_mate(r))

        each(0, PLANE, one)

    for r in range(1, PLANE):
        row_copy(r, from_mate(r)).wait_recv()
    keep_table.start()
    for w in range(2):
        for far in (1, 2):
            table_copy(w, far).start()
    keep_inverse.wait()
    keep_table.wait()
    for t in range(2):
        choose(0, t, lambda spot: own[t][spot])
        spread(0, t)

    each(1, PLANE, lambda r: g1(r, mate(r)).wait_recv())
    total = g_in[0]
    for r in range(1, PLANE):
        total = total + g_in[r]
    g_part[...] = total
    each(1, LAYERS, lambda s: g2(s).start())
    g_col[0] = total

    attend_layer(0)

    for t in range(2):
        for w in range(2):
            hop1(w, t).wait_recv()
            hop2(w, t).start()
        for w in range(2):
            choose(1 + w, t, lambda spot: first_hop[w][t][spot])
            spread(1 + w, t)

    each(1, LAYERS, lambda s: g2(s).wait_recv())
    total = g_col[0]
    for s in range(1, LAYERS):
        total = total + g_col[s]
    g_sum[...] = total
    each(1, PLANE, lambda r: g3(r, mate(r), p_me).start())
    g_all[piece_at(p_me), :] = total

    for side in range(2):
        for t in range(2):
            halo_copy(side, t).wait_recv()
    pads = (key_pad, value_pad)
    for t in range(2):
        pads[t][pl.ds(0, BLOCK), :] = halo[0, pl.ds(t * BLOCK, BLOCK), :]
        pads[t][pl.ds(BLOCK, tokens), :] = own[t][...].reshape(tokens, width)
        pads[t][pl.ds(BLOCK + tokens, BLOCK), :] = halo[1, pl.ds(t * BLOCK, BLOCK), :]
    each(1, PLANE, lambda r: g3(r, mate(r), from_mate(r)).wait_recv())

    tile = 2 * BLOCK
    span = tile + 2 * BLOCK
    steps = tokens // tile

    def near(step):
        wide = span + G * BLOCK
        row_block = lax.broadcasted_iota(jnp.int32, (tile, wide), 0) // BLOCK
        column = lax.broadcasted_iota(jnp.int32, (tile, wide), 1)
        key_block = column // BLOCK
        first = jnp.where((me == 0) & (step == 0), 1, 0)
        last = jnp.where((me == count - 1) & (step == steps - 1), 1, 0)
        listed = (key_block >= row_block) & (key_block <= row_block + 2)
        listed = listed & (key_block >= first) & (key_block < span // BLOCK - last)
        listed = listed | (column >= span)
        rows = pl.ds(pl.multiple_of(step * tile, tile), tile)
        around = pl.ds(pl.multiple_of(step * tile, tile), span)
        maxima, sums = [], []
        for h in range(heads):
            shared = [g_all[pl.ds(b * BLOCK, BLOCK), columns(h)] for b in range(2 * G)]
            keys = jnp.concatenate([key_pad[around, columns(h)]] + shared[0::2], axis=0)
            values = jnp.concatenate([value_pad[around, columns(h)]] + shared[1::2], axis=0)
            query = q_ref[pl.ds(step * (tile // BLOCK), tile // BLOCK), :, columns(h)].reshape(tile, HD)
            scores = lax.dot_general(query, keys, NT, preferred_element_type=jnp.float32)
            scores = jnp.where(listed, scores * HD**-0.5, LOW)
            row_max = jnp.max(scores, axis=1, keepdims=True)
            lifted = jnp.exp(scores - row_max)
            maxima.append(row_max)
            sums.append(jnp.sum(lifted, axis=1, keepdims=True))
            near_acc[rows, columns(h)] = jnp.dot(
                lifted.astype(jnp.bfloat16), values, preferred_element_type=jnp.float32
            )
        near_max[rows, :] = lanes_of(maxima)
        near_sum[rows, :] = lanes_of(sums)

    each(0, steps, near)
    for w in range(2):
        attend_layer(1 + w)

    for w in range(2):
        for far in (1, 2):
            table_copy(w, far).wait_recv()
    keep_tables.start()
    keep_tables.wait()
    for t in range(2):
        for w in range(2):
            hop2(w, t).wait_recv()
            owner = col(-2 * ways[w])

            def one(j, r, far):
                pick3[w, t, j] = second_hop[w][t][tables[2 * w + far - 1, mate(r), 0, owner]]

            each(0, 4, lambda j: one(j, 2 * j + w, 2))
            hop3(w, t, 0).start()
            each(0, PLANE, lambda r: one(4 + r, r, 1))
            for c in (1, 2):
                hop3(w, t, c).start()
        for w in range(2):
            choose(3 + w, t, lambda spot: second_hop[w][t][spot])
            spread(3 + w, t)
    for t in range(2):
        for w in range(2):
            hop3(w, t, 0).wait_recv()
            for j in range(4):
                (hop4 if 2 * j + w == 0 else relay)(w, t, j).start()
        for c in (1, 2):
            for w in range(2):
                hop3(w, t, c).wait_recv()
                for r in range(4 * c - 4, 4 * c):
                    if r == 0:
                        fetched[t, layer(5 + w) * PLANE + p_me] = got3[w, t, 4]
                    else:
                        spread_one(5 + w, t, r, got3.at[w, t, 4 + r]).start()
            if c == 1:
                for w in range(2):
                    for j in range(4):
                        if 2 * j + w > 0:
                            relay(w, t, j).wait_recv()
                            hop4(w, t, j).start()
        if t == 0:
            for f in (1, 3, 2):
                row_weight(f, lax.rem(row - f + 4, 4)).wait_recv()
                core_weight(f, part_rows).start()
            for w in range(2):
                attend_layer(3 + w)
    attend_layer(5)
    attend_layer(6)
    for w in range(2):
        for j in range(4):
            for t in range(2):
                last_arrived(w, t, j)
            attend(layer(7) * PLANE + from_mate(2 * j + w))

    quarter = tokens // 4

    def merge(block):
        rows = pl.ds(pl.multiple_of(block * BLOCK, BLOCK), BLOCK)
        slots = [lax.div(ids[block, j], blocks_here) for j in range(R)]
        maxima = [near_max[rows, :]] + [far_max[slot] for slot in slots]
        top = maxima[0]
        for one in maxima[1:]:
            top = jnp.maximum(top, one)
        scales = [jnp.exp(one - top) for one in maxima]
        sums = [near_sum[rows, :]] + [far_sum[slot] for slot in slots]
        whole = scales[0] * sums[0]
        for scale, one in zip(scales[1:], sums[1:]):
            whole = whole + scale * one
        scales = [scale / whole for scale in scales]
        for h in range(heads):
            out = scales[0][:, h : h + 1] * near_acc[rows, columns(h)]
            for scale, slot in zip(scales[1:], slots):
                out = out + scale[:, h : h + 1] * far_acc[slot, :, columns(h)]
            context[rows, columns(h)] = out.astype(jnp.bfloat16)

    def quarter_at(f):
        return pl.ds(pl.multiple_of(f * quarter, quarter), quarter)

    def heads_at(f):
        return pl.ds(pl.multiple_of(f * width, width), width)

    blocks = quarter // BLOCK
    for f in (2, 1, 3, 0):
        to = lax.rem(row + f, 4)
        each(0, blocks, lambda b: merge(to * blocks + b))
        if f > 0:
            cross(context.at[quarter_at(to)], heads_ref.at[:, heads_at(row)], c_s.at[f], c_r.at[f], to).start()
        else:
            heads_ref[:, heads_at(row)] = context[quarter_at(row), :]

    for t in range(2):
        for w in range(2):
            hop1(w, t).wait_send()
            hop2(w, t).wait_send()
            for c in range(3):
                hop3(w, t, c).wait_send()
            for j in range(4):
                if 2 * j + w > 0:
                    relay(w, t, j).wait_send()
                hop4(w, t, j).wait_send()
    for side in range(2):
        for t in range(2):
            halo_copy(side, t).wait_send()
    for d in range(LAYERS - 1):
        for t in range(2):
            each(1, PLANE, lambda r: spread_one(d, t, r, fetched.at[t, 0]).wait_send())
    each(1, PLANE, lambda r: g1(r, mate(r)).wait_send())
    each(1, LAYERS, lambda s: g2(s).wait_send())
    each(1, PLANE, lambda r: g3(r, mate(r), p_me).wait_send())
    for r in range(1, PLANE):
        row_copy(r, p_me).wait_send()
    for w in range(2):
        for far in (1, 2):
            table_copy(w, far).wait_send()
    own_weight.wait()
    other_rows = pl.ds(pl.multiple_of((1 - core) * (depth // 2), depth // 2), depth // 2)
    for f in range(1, 4):
        row_weight(f, row).wait_send()
        core_weight(f, part_rows).wait_send()
        core_weight(f, other_rows).wait_recv()
    for f in range(1, 4):
        cross(context.at[quarter_at(0)], heads_ref.at[:, heads_at(row)], c_s.at[f], c_r.at[f], row).wait_send()
        came = lax.rem(row - f + 4, 4)
        cross(context.at[quarter_at(0)], heads_ref.at[:, heads_at(came)], c_s.at[f], c_r.at[f], row).wait_recv()


def gather_attend(ids, shared_ids, query, keys, values, weight):
    tokens, width = query.shape[0] * BLOCK, query.shape[2]
    n = PLANE * LAYERS
    pair = 2 * BLOCK
    piece = G * pair // PLANE
    half, full = jnp.bfloat16, jnp.float32
    vmem = pl.BlockSpec(memory_space=pltpu.VMEM)
    smem = pl.BlockSpec(memory_space=pltpu.SMEM)
    sem = pltpu.SemaphoreType.DMA
    hop = pltpu.VMEM(query.shape, half)
    return pl.pallas_call(
        kernel,
        out_shape=[
            jax.ShapeDtypeStruct((tokens // 4, 4 * width), half),
            jax.ShapeDtypeStruct((4,) + weight.shape, half),
        ],
        in_specs=[smem] * 2 + [vmem] * 3 + [pl.BlockSpec(memory_space=pl.ANY)],
        out_specs=[vmem, pl.BlockSpec(memory_space=pl.ANY)],
        scratch_shapes=[
            pltpu.VMEM((2, n, BLOCK, width), half),
            hop, hop, hop, hop, hop, hop, hop, hop,
            pltpu.VMEM((5, 2, PLANE, BLOCK, width), half),
            pltpu.VMEM((2, 2, 12, BLOCK, width), half),
            pltpu.VMEM((2, 2, 12, BLOCK, width), half),
            pltpu.VMEM((2, 2, 4, BLOCK, width), half),
            pltpu.VMEM((2, pair, width), half),
            pltpu.VMEM((tokens + pair, width), half),
            pltpu.VMEM((tokens + pair, width), half),
            pltpu.VMEM((G * pair, width), half),
            pltpu.VMEM((PLANE, piece, width), half),
            pltpu.VMEM((piece, width), half),
            pltpu.VMEM((LAYERS, piece, width), half),
            pltpu.VMEM((piece, width), half),
            pltpu.VMEM((G * pair, width), half),
            pltpu.VMEM((tokens, width), full),
            pltpu.VMEM((tokens, HD), full),
            pltpu.VMEM((tokens, HD), full),
            pltpu.VMEM((n, BLOCK, width), full),
            pltpu.VMEM((n, BLOCK, HD), full),
            pltpu.VMEM((n, BLOCK, HD), full),
            pltpu.VMEM((tokens, width), half),
            pltpu.VMEM((PLANE, HD), jnp.int32),
            pltpu.VMEM((PLANE, HD), jnp.int32),
            pltpu.VMEM((PLANE, PLANE, HD), jnp.int32),
            pltpu.VMEM((4, PLANE, PLANE, HD), jnp.int32),
            pltpu.SMEM((PLANE, HD), jnp.int32),
            pltpu.SMEM((PLANE, PLANE, HD), jnp.int32),
            pltpu.SMEM((4, PLANE, PLANE, HD), jnp.int32),
            sem((2, 2)), sem((2, 2)), sem((2, 2)), sem((2, 2)),
            sem((2, 2, 3)), sem((2, 2, 3)), sem((2, 2, 4)), sem((2, 2, 4)), sem((2, 2, 4)), sem((2, 2, 4)),
            sem((2, LAYERS, PLANE)), sem((2, LAYERS, PLANE)),
            sem((2, 2)), sem((2, 2)), sem((3, 8)), sem((3, 8)), sem((4,)), sem((4,)),
            sem((PLANE,)), sem((PLANE,)), sem((4,)), sem((4,)), sem((4,)),
            sem((4,)), sem((4,)), sem((4,)), sem((4,)),
        ],
        compiler_params=pltpu.CompilerParams(
            collective_id=0, has_side_effects=True, vmem_limit_bytes=58 << 20
        ),
        cost_estimate=pl.CostEstimate(flops=3 * 10**9, bytes_accessed=10 * 10**6, transcendentals=4 * 10**6),
    )(ids, shared_ids, query, keys, values, weight)


def project_kernel(heads_ref, weight_ref, out_ref):
    product = jnp.dot(heads_ref[...], weight_ref[...], preferred_element_type=jnp.float32)
    out_ref[...] = product.astype(out_ref.dtype)


def project(heads, weight):
    rows, depth = heads.shape
    columns = weight.shape[1]
    tile = 512
    return pl.pallas_call(
        project_kernel,
        grid=(columns // tile,),
        in_specs=[
            pl.BlockSpec((rows, depth), lambda i: (0, 0)),
            pl.BlockSpec((depth, tile), lambda i: (0, i)),
        ],
        out_specs=pl.BlockSpec((rows, tile), lambda i: (0, i)),
        out_shape=jax.ShapeDtypeStruct((rows, columns), heads.dtype),
        compiler_params=pltpu.CompilerParams(vmem_limit_bytes=40 << 20),
    )(heads, weight)


def on_device(query_rows, key_rows, value_rows, out_weight, random_ids, global_ids):
    tokens, width = query_rows.shape
    blocks = tokens // BLOCK
    rows = [array.reshape(blocks, BLOCK, width) for array in (query_rows, key_rows, value_rows)]
    all_heads, weight = gather_attend(random_ids, global_ids, *rows, out_weight)
    weight = weight.reshape(-1, out_weight.shape[1])
    return project(all_heads, weight)


def solution(mesh):
    return jax.shard_map(
        on_device,
        mesh=mesh,
        in_specs=(
            P("seq", "fsdp"),
            P("seq", "fsdp"),
            P("seq", "fsdp"),
            P("fsdp", None),
            P("seq", None),
            P(),
        ),
        out_specs=P(("seq", "fsdp"), None),
        check_vma=False,
    )
```

```python
import jax
import jax.numpy as jnp
from jax import lax
from jax.experimental import pallas as pl
from jax.experimental.pallas import tpu as pltpu
from jax.sharding import PartitionSpec as P

HD = 128
BLOCK = 64
G = 2
R = 3
LOW = -1e30
NT = (((1,), (1,)), ((), ()))
MESH = pl.DeviceIdType.MESH
PLANE = 8
LAYERS = 8
SHIFTS = (0, 1, -1, 2, -2, 3, -3, 4)


def lanes_of(parts):
    rows = parts[0].shape[0]
    lane = lax.broadcasted_iota(jnp.int32, (rows, HD), 1)
    out = jnp.zeros((rows, HD), jnp.float32)
    for i, part in enumerate(parts):
        out = jnp.where(lane == i, part, out)
    return out


def kernel(
    ids, shared_ids,
    q_ref, k_ref, v_ref, w_ref,
    out_ref, weight_ref,
    result, heads_in, fetched,
    front1_k, front1_v, back1_k, back1_v, front2_k, front2_v, back2_k, back2_v, stage, pick3, got3, got4,
    halo, key_pad, value_pad, g_mine, g_in, g_part, g_col, g_sum, g_all,
    near_acc, near_max, near_sum, far_acc, far_max, far_sum, context,
    mine_v, inverse_v, table_v, tables_v, inverse, table, tables,
    hop1_s, hop1_r, hop2_s, hop2_r, hop3_s, hop3_r, hop4_s, hop4_r, relay_s, relay_r,
    in_s, in_r, halo_s, halo_r, g_s, g_r, c_s, c_r, t_s, t_r, far_s, far_r, local_s,
    row_s, row_r, core_s, core_r, load_s, out_s,
):
    me = lax.axis_index("seq")
    row = lax.axis_index("fsdp")
    z, p_me = me // PLANE, me % PLANE
    count = PLANE * LAYERS
    tokens, width = key_pad.shape[0] - 2 * BLOCK, q_ref.shape[2]
    heads = width // HD
    pair = 2 * BLOCK

    def col(shift):
        return lax.rem(z + shift + LAYERS, LAYERS) * PLANE + p_me

    def mate(r):
        return lax.rem(p_me + r, PLANE)

    def from_mate(r):
        return lax.rem(p_me - r + PLANE, PLANE)

    def layer(d):
        return lax.rem(z - SHIFTS[d] + LAYERS, LAYERS)

    def copy(src, dst, send, recv, device):
        return pltpu.make_async_remote_copy(
            src_ref=src, dst_ref=dst, send_sem=send, recv_sem=recv,
            device_id={"seq": device}, device_id_type=MESH,
        )

    def cross(src, dst, send, recv, device):
        return pltpu.make_async_remote_copy(
            src_ref=src, dst_ref=dst, send_sem=send, recv_sem=recv,
            device_id={"fsdp": device}, device_id_type=MESH,
        )

    next_one, last_one = lax.rem(me + 1, count), lax.rem(me + count - 1, count)
    barrier = pltpu.get_barrier_semaphore()
    for r in range(1, PLANE):
        pl.semaphore_signal(barrier, inc=1, device_id={"seq": z * PLANE + mate(r)}, device_id_type=MESH)
    for s in range(1, LAYERS):
        pl.semaphore_signal(barrier, inc=1, device_id={"seq": col(s)}, device_id_type=MESH)
    pl.semaphore_signal(barrier, inc=1, device_id={"seq": next_one}, device_id_type=MESH)
    pl.semaphore_signal(barrier, inc=1, device_id={"seq": last_one}, device_id_type=MESH)
    for f in range(1, 4):
        pl.semaphore_signal(barrier, inc=1, device_id={"fsdp": lax.rem(row + f, 4)}, device_id_type=MESH)
    pl.semaphore_wait(barrier, 7 + 7 + 2 + 3)

    ways = (1, -1)
    first_hop = ((front1_k, front1_v), (back1_k, back1_v))
    second_hop = ((front2_k, front2_v), (back2_k, back2_v))
    own = (k_ref, v_ref)

    def hop1(w, t):
        return copy(own[t], first_hop[w][t], hop1_s.at[w, t], hop1_r.at[w, t], col(ways[w]))

    def hop2(w, t):
        return copy(first_hop[w][t], second_hop[w][t], hop2_s.at[w, t], hop2_r.at[w, t], col(ways[w]))

    def hop3(w, t, c):
        part = pl.ds(4 * c, 4)
        return copy(
            pick3.at[w, t, part], got3.at[w, t, part], hop3_s.at[w, t, c], hop3_r.at[w, t, c], col(ways[w])
        )

    def relay(w, t, j):
        return copy(
            got3.at[w, t, j], got4.at[w, t, j], relay_s.at[w, t, j], relay_r.at[w, t, j],
            z * PLANE + mate(2 * j + w),
        )

    def hop4(w, t, j):
        src = got3.at[w, t, j] if 2 * j + w == 0 else got4.at[w, t, j]
        owner = col(-3 * ways[w]) - p_me + from_mate(2 * j + w)
        return copy(src, fetched.at[t, owner], hop4_s.at[w, t, j], hop4_r.at[w, t, j], col(ways[w]))

    def last_arrived(w, t, j):
        spot = fetched.at[t, layer(7) * PLANE + from_mate(2 * j + w)]
        copy(spot, spot, hop4_s.at[w, t, j], hop4_r.at[w, t, j], col(ways[w])).wait_recv()

    core = lax.rem(me, 2)
    depth = w_ref.shape[0]
    part_rows = pl.ds(core * (depth // 2), depth // 2)

    def row_weight(f, at):
        return cross(
            w_ref.at[part_rows], weight_ref.at[at, part_rows], row_s.at[f], row_r.at[f], lax.rem(row + f, 4)
        )

    def core_weight(f, rows):
        came = lax.rem(row - f + 4, 4)
        return copy(
            weight_ref.at[came, rows], weight_ref.at[came, rows], core_s.at[f], core_r.at[f], me + 1 - 2 * core
        )

    other_rows = pl.ds((1 - core) * (depth // 2), depth // 2)
    chunk = 512
    chunks = w_ref.shape[2] // chunk

    def place(k, i):
        if k < 2:
            return (second_hop, first_hop)[k][i // 4][i // 2 % 2].at[pl.ds(depth * (i % 2), depth)]
        if k == 2:
            return stage.at[i // 2, i % 2]
        return (pick3, got3)[i // 4].at[i // 2 % 2, i % 2, pl.ds(0, depth)]

    def load(k, i):
        columns_i = pl.ds(i * chunk, chunk)
        if k == 0:
            src = w_ref.at[:, :, columns_i]
        else:
            src = weight_ref.at[lax.rem(row - k + 4, 4), :, :, columns_i]
        return pltpu.make_async_copy(src, place(k, i), load_s.at[k, i])

    def load_all(k):
        for i in range(chunks):
            load(k, i).start()

    for t in range(2):
        for w in range(2):
            hop1(w, t).start()
    for f in (1, 3, 2):
        row_weight(f, row).start()

    def halo_copy(side, t):
        block = tokens // BLOCK - 1 if side == 0 else 0
        return copy(
            own[t].at[block], halo.at[side, pl.ds(t * BLOCK, BLOCK)], halo_s.at[side, t], halo_r.at[side, t],
            next_one if side == 0 else last_one,
        )

    for side in range(2):
        for t in range(2):
            halo_copy(side, t).start()

    blocks_here = ids.shape[0]
    lane = lax.broadcasted_iota(jnp.int32, mine_v.shape, 1)
    wanted = jnp.zeros(mine_v.shape, jnp.int32)
    askers = jnp.zeros(mine_v.shape, jnp.int32)
    for b in range(blocks_here):
        for j in range(R):
            hit = lane == lax.div(ids[b, j], blocks_here)
            wanted = jnp.where(hit, lax.rem(ids[b, j], blocks_here), wanted)
            askers = jnp.where(hit, b, askers)
    mine_v[...] = wanted
    inverse_v[...] = askers

    def row_copy(r, at):
        return copy(mine_v, table_v.at[at], t_s.at[r], t_r.at[r], z * PLANE + mate(r))

    def table_copy(w, far):
        k = 2 * w + far - 1
        return copy(table_v, tables_v.at[k], far_s.at[k], far_r.at[k], col(-far * ways[w]))

    for r in range(1, PLANE):
        row_copy(r, p_me).start()
    table_v[p_me] = wanted
    keep_inverse = pltpu.make_async_copy(inverse_v, inverse, local_s.at[0])
    keep_table = pltpu.make_async_copy(table_v, table, local_s.at[1])
    keep_tables = pltpu.make_async_copy(tables_v, tables, local_s.at[2])
    keep_inverse.start()

    piece = G * pair // PLANE
    for g in range(G):
        holder = jnp.full((BLOCK, width), lax.div(shared_ids[g], blocks_here), jnp.int32)
        keep = jnp.where(holder == me, 1.0, 0.0)
        for t in range(2):
            block = own[t][lax.rem(shared_ids[g], blocks_here)].astype(jnp.float32) * keep
            g_mine[pl.ds(g * pair + t * BLOCK, BLOCK), :] = block.astype(jnp.bfloat16)

    def piece_at(p):
        return pl.ds(pl.multiple_of(p * piece, piece), piece)

    def g1(r, p):
        return copy(g_mine.at[piece_at(p)], g_in.at[r], g_s.at[0, r], g_r.at[0, r], z * PLANE + p)

    def g2(s):
        return copy(g_part, g_col.at[s], g_s.at[1, s], g_r.at[1, s], col(s))

    def g3(r, p, at):
        return copy(g_sum, g_all.at[piece_at(at)], g_s.at[2, r], g_r.at[2, r], z * PLANE + p)

    def each(low, high, body):
        def step(i, carry):
            body(i)
            return carry

        lax.fori_loop(low, high, step, 0)

    each(1, PLANE, lambda r: g1(r, mate(r)).start())
    g_in[0] = g_mine[piece_at(p_me), :]

    def choose(d, t, read):
        owner = layer(d) * PLANE + p_me

        def one(r):
            stage[d, t, r] = read(table[mate(r), 0, owner])

        each(0, PLANE, one)
        fetched[t, owner] = stage[d, t, 0]

    def spread_one(d, t, r, src):
        owner = layer(d) * PLANE + p_me
        return copy(src, fetched.at[t, owner], in_s.at[t, d, r], in_r.at[t, d, r], z * PLANE + mate(r))

    def spread(d, t):
        each(1, PLANE, lambda r: spread_one(d, t, r, stage.at[d, t, r]).start())

    def arrived(d, r):
        owner = layer(d) * PLANE + from_mate(r)
        for t in range(2):
            spot = fetched.at[t, owner]
            copy(spot, spot, in_s.at[t, d, r], in_r.at[t, d, r], z * PLANE + mate(r)).wait_recv()

    def columns(h):
        return pl.ds(h * HD, HD)

    def attend(owner):
        asker = inverse[0, owner]
        scores = []
        for h in range(heads):
            keys = fetched[0, owner, :, columns(h)]
            scores.append(lax.dot_general(q_ref[asker, :, columns(h)], keys, NT, preferred_element_type=jnp.float32))
        scores = jnp.concatenate(scores, axis=0) * HD**-0.5
        row_max = jnp.max(scores, axis=1, keepdims=True)
        lifted = jnp.exp(scores - row_max)
        row_sum = jnp.sum(lifted, axis=1, keepdims=True)
        lifted = lifted.astype(jnp.bfloat16)
        parts = [slice(h * BLOCK, (h + 1) * BLOCK) for h in range(heads)]
        for h in range(heads):
            values = fetched[1, owner, :, columns(h)]
            far_acc[owner, :, columns(h)] = jnp.dot(lifted[parts[h]], values, preferred_element_type=jnp.float32)
        far_max[owner] = lanes_of([row_max[part] for part in parts])
        far_sum[owner] = lanes_of([row_sum[part] for part in parts])

    def attend_layer(d):
        def one(r):
            @pl.when(r > 0)
            def _():
                arrived(d, r)

            attend(layer(d) * PLANE + from_mate(r))

        each(0, PLANE, one)

    for r in range(1, PLANE):
        row_copy(r, from_mate(r)).wait_recv()
    keep_table.start()
    for w in range(2):
        for far in (1, 2):
            table_copy(w, far).start()
    keep_inverse.wait()
    keep_table.wait()
    for t in range(2):
        choose(0, t, lambda spot: own[t][spot])
        spread(0, t)

    each(1, PLANE, lambda r: g1(r, mate(r)).wait_recv())
    total = g_in[0]
    for r in range(1, PLANE):
        total = total + g_in[r]
    g_part[...] = total
    each(1, LAYERS, lambda s: g2(s).start())
    g_col[0] = total

    attend_layer(0)

    for t in range(2):
        for w in range(2):
            hop1(w, t).wait_recv()
            hop2(w, t).start()
        for w in range(2):
            choose(1 + w, t, lambda spot: first_hop[w][t][spot])
            spread(1 + w, t)

    each(1, LAYERS, lambda s: g2(s).wait_recv())
    total = g_col[0]
    for s in range(1, LAYERS):
        total = total + g_col[s]
    g_sum[...] = total
    each(1, PLANE, lambda r: g3(r, mate(r), p_me).start())
    g_all[piece_at(p_me), :] = total

    for side in range(2):
        for t in range(2):
            halo_copy(side, t).wait_recv()
    pads = (key_pad, value_pad)
    for t in range(2):
        pads[t][pl.ds(0, BLOCK), :] = halo[0, pl.ds(t * BLOCK, BLOCK), :]
        pads[t][pl.ds(BLOCK, tokens), :] = own[t][...].reshape(tokens, width)
        pads[t][pl.ds(BLOCK + tokens, BLOCK), :] = halo[1, pl.ds(t * BLOCK, BLOCK), :]
    each(1, PLANE, lambda r: g3(r, mate(r), from_mate(r)).wait_recv())

    tile = 2 * BLOCK
    span = tile + 2 * BLOCK
    steps = tokens // tile

    def near(step):
        wide = span + G * BLOCK
        row_block = lax.broadcasted_iota(jnp.int32, (tile, wide), 0) // BLOCK
        column = lax.broadcasted_iota(jnp.int32, (tile, wide), 1)
        key_block = column // BLOCK
        first = jnp.where((me == 0) & (step == 0), 1, 0)
        last = jnp.where((me == count - 1) & (step == steps - 1), 1, 0)
        listed = (key_block >= row_block) & (key_block <= row_block + 2)
        listed = listed & (key_block >= first) & (key_block < span // BLOCK - last)
        listed = listed | (column >= span)
        rows = pl.ds(pl.multiple_of(step * tile, tile), tile)
        around = pl.ds(pl.multiple_of(step * tile, tile), span)
        maxima, sums = [], []
        for h in range(heads):
            shared = [g_all[pl.ds(b * BLOCK, BLOCK), columns(h)] for b in range(2 * G)]
            keys = jnp.concatenate([key_pad[around, columns(h)]] + shared[0::2], axis=0)
            values = jnp.concatenate([value_pad[around, columns(h)]] + shared[1::2], axis=0)
            query = q_ref[pl.ds(step * (tile // BLOCK), tile // BLOCK), :, columns(h)].reshape(tile, HD)
            scores = lax.dot_general(query, keys, NT, preferred_element_type=jnp.float32)
            scores = jnp.where(listed, scores * HD**-0.5, LOW)
            row_max = jnp.max(scores, axis=1, keepdims=True)
            lifted = jnp.exp(scores - row_max)
            maxima.append(row_max)
            sums.append(jnp.sum(lifted, axis=1, keepdims=True))
            near_acc[rows, columns(h)] = jnp.dot(
                lifted.astype(jnp.bfloat16), values, preferred_element_type=jnp.float32
            )
        near_max[rows, :] = lanes_of(maxima)
        near_sum[rows, :] = lanes_of(sums)

    each(0, steps, near)
    for w in range(2):
        attend_layer(1 + w)

    for w in range(2):
        for far in (1, 2):
            table_copy(w, far).wait_recv()
    keep_tables.start()
    keep_tables.wait()
    for t in range(2):
        for w in range(2):
            hop2(w, t).wait_recv()
            owner = col(-2 * ways[w])

            def one(j, r, far):
                pick3[w, t, j] = second_hop[w][t][tables[2 * w + far - 1, mate(r), 0, owner]]

            each(0, 4, lambda j: one(j, 2 * j + w, 2))
            hop3(w, t, 0).start()
            each(0, PLANE, lambda r: one(4 + r, r, 1))
            for c in (1, 2):
                hop3(w, t, c).start()
        for w in range(2):
            choose(3 + w, t, lambda spot: second_hop[w][t][spot])
            spread(3 + w, t)
    for t in range(2):
        for w in range(2):
            hop3(w, t, 0).wait_recv()
            for j in range(4):
                (hop4 if 2 * j + w == 0 else relay)(w, t, j).start()
        for c in (1, 2):
            for w in range(2):
                hop3(w, t, c).wait_recv()
                for r in range(4 * c - 4, 4 * c):
                    if r == 0:
                        fetched[t, layer(5 + w) * PLANE + p_me] = got3[w, t, 4]
                    else:
                        spread_one(5 + w, t, r, got3.at[w, t, 4 + r]).start()
            if c == 1:
                for w in range(2):
                    for j in range(4):
                        if 2 * j + w > 0:
                            relay(w, t, j).wait_recv()
                            hop4(w, t, j).start()
        if t == 0:
            for f in (1, 3, 2):
                row_weight(f, lax.rem(row - f + 4, 4)).wait_recv()
                core_weight(f, part_rows).start()
            for w in range(2):
                attend_layer(3 + w)
            load_all(0)
    attend_layer(5)
    attend_layer(6)
    for w in range(2):
        for t in range(2):
            hop2(w, t).wait_send()
    for f in range(1, 4):
        core_weight(f, other_rows).wait_recv()
    load_all(1)
    for d in range(5):
        for t in range(2):
            each(1, PLANE, lambda r: spread_one(d, t, r, fetched.at[t, 0]).wait_send())
    load_all(2)
    for w in range(2):
        for j in range(4):
            for t in range(2):
                last_arrived(w, t, j)
            attend(layer(7) * PLANE + from_mate(2 * j + w))

    quarter = tokens // 4

    def merge(block):
        rows = pl.ds(pl.multiple_of(block * BLOCK, BLOCK), BLOCK)
        slots = [lax.div(ids[block, j], blocks_here) for j in range(R)]
        maxima = [near_max[rows, :]] + [far_max[slot] for slot in slots]
        top = maxima[0]
        for one in maxima[1:]:
            top = jnp.maximum(top, one)
        scales = [jnp.exp(one - top) for one in maxima]
        sums = [near_sum[rows, :]] + [far_sum[slot] for slot in slots]
        whole = scales[0] * sums[0]
        for scale, one in zip(scales[1:], sums[1:]):
            whole = whole + scale * one
        scales = [scale / whole for scale in scales]
        for h in range(heads):
            out = scales[0][:, h : h + 1] * near_acc[rows, columns(h)]
            for scale, slot in zip(scales[1:], slots):
                out = out + scale[:, h : h + 1] * far_acc[slot, :, columns(h)]
            context[rows, columns(h)] = out.astype(jnp.bfloat16)

    def quarter_at(f):
        return pl.ds(pl.multiple_of(f * quarter, quarter), quarter)

    def exchange(f):
        to = lax.rem(row + f, 4)
        return cross(context.at[quarter_at(to)], heads_in.at[f], c_s.at[f], c_r.at[f], to)

    for t in range(2):
        for w in range(2):
            for c in range(3):
                hop3(w, t, c).wait_send()
            for j in range(4):
                if 2 * j + w > 0:
                    relay(w, t, j).wait_send()
                else:
                    hop4(w, t, j).wait_send()
            each(1, PLANE, lambda r: spread_one(5 + w, t, r, fetched.at[t, 0]).wait_send())
    load_all(3)

    blocks = quarter // BLOCK
    for f in (2, 1, 3, 0):
        to = lax.rem(row + f, 4)
        each(0, blocks, lambda b: merge(to * blocks + b))
        if f > 0:
            exchange(f).start()

    def tile_of(k, i):
        return place(k, i)[...].reshape(depth * BLOCK, chunk)

    group = quarter // BLOCK

    def product(block, k, i):
        return jnp.dot(block, tile_of(k, i), preferred_element_type=jnp.float32)

    mine = context[quarter_at(row), :]
    for i in range(chunks):
        load(0, i).wait()
        far_acc[pl.ds(group * i, group)] = product(mine, 0, i).reshape(group, BLOCK, chunk)
    for f in (2, 1, 3):
        exchange(f).wait_recv()

    def write(i):
        columns_i = pl.ds(i * chunk, chunk)
        return pltpu.make_async_copy(result.at[:, columns_i], out_ref.at[:, columns_i], out_s.at[i])

    for i in range(chunks):
        part = far_acc[pl.ds(group * i, group)].reshape(quarter, chunk)
        for f in (1, 2, 3):
            load(f, i).wait()
            part = part + product(heads_in[f], f, i)
        result[:, pl.ds(i * chunk, chunk)] = part.astype(jnp.bfloat16)
        write(i).start()

    for t in range(2):
        for w in range(2):
            hop1(w, t).wait_send()
            for j in range(4):
                if 2 * j + w > 0:
                    hop4(w, t, j).wait_send()
    for side in range(2):
        for t in range(2):
            halo_copy(side, t).wait_send()
    each(1, PLANE, lambda r: g1(r, mate(r)).wait_send())
    each(1, LAYERS, lambda s: g2(s).wait_send())
    each(1, PLANE, lambda r: g3(r, mate(r), p_me).wait_send())
    for r in range(1, PLANE):
        row_copy(r, p_me).wait_send()
    for w in range(2):
        for far in (1, 2):
            table_copy(w, far).wait_send()
    for f in range(1, 4):
        row_weight(f, row).wait_send()
        core_weight(f, part_rows).wait_send()
        exchange(f).wait_send()
    for i in range(chunks):
        write(i).wait()


def gather_attend(ids, shared_ids, query, keys, values, weight):
    tokens, width = query.shape[0] * BLOCK, query.shape[2]
    n = PLANE * LAYERS
    pair = 2 * BLOCK
    piece = G * pair // PLANE
    half, full = jnp.bfloat16, jnp.float32
    vmem = pl.BlockSpec(memory_space=pltpu.VMEM)
    smem = pl.BlockSpec(memory_space=pltpu.SMEM)
    sem = pltpu.SemaphoreType.DMA
    hop = pltpu.VMEM(query.shape, half)
    return pl.pallas_call(
        kernel,
        out_shape=[
            jax.ShapeDtypeStruct((tokens // 4, weight.shape[2]), half),
            jax.ShapeDtypeStruct((4,) + weight.shape, half),
        ],
        in_specs=[smem] * 2 + [vmem] * 3 + [pl.BlockSpec(memory_space=pl.ANY)],
        out_specs=[pl.BlockSpec(memory_space=pl.ANY)] * 2,
        scratch_shapes=[
            pltpu.VMEM((tokens // 4, weight.shape[2]), half),
            pltpu.VMEM((4, tokens // 4, width), half),
            pltpu.VMEM((2, n, BLOCK, width), half),
            hop, hop, hop, hop, hop, hop, hop, hop,
            pltpu.VMEM((5, 2, PLANE, BLOCK, width), half),
            pltpu.VMEM((2, 2, 12, BLOCK, width), half),
            pltpu.VMEM((2, 2, 12, BLOCK, width), half),
            pltpu.VMEM((2, 2, 4, BLOCK, width), half),
            pltpu.VMEM((2, pair, width), half),
            pltpu.VMEM((tokens + pair, width), half),
            pltpu.VMEM((tokens + pair, width), half),
            pltpu.VMEM((G * pair, width), half),
            pltpu.VMEM((PLANE, piece, width), half),
            pltpu.VMEM((piece, width), half),
            pltpu.VMEM((LAYERS, piece, width), half),
            pltpu.VMEM((piece, width), half),
            pltpu.VMEM((G * pair, width), half),
            pltpu.VMEM((tokens, width), full),
            pltpu.VMEM((tokens, HD), full),
            pltpu.VMEM((tokens, HD), full),
            pltpu.VMEM((n, BLOCK, width), full),
            pltpu.VMEM((n, BLOCK, HD), full),
            pltpu.VMEM((n, BLOCK, HD), full),
            pltpu.VMEM((tokens, width), half),
            pltpu.VMEM((PLANE, HD), jnp.int32),
            pltpu.VMEM((PLANE, HD), jnp.int32),
            pltpu.VMEM((PLANE, PLANE, HD), jnp.int32),
            pltpu.VMEM((4, PLANE, PLANE, HD), jnp.int32),
            pltpu.SMEM((PLANE, HD), jnp.int32),
            pltpu.SMEM((PLANE, PLANE, HD), jnp.int32),
            pltpu.SMEM((4, PLANE, PLANE, HD), jnp.int32),
            sem((2, 2)), sem((2, 2)), sem((2, 2)), sem((2, 2)),
            sem((2, 2, 3)), sem((2, 2, 3)), sem((2, 2, 4)), sem((2, 2, 4)), sem((2, 2, 4)), sem((2, 2, 4)),
            sem((2, LAYERS, PLANE)), sem((2, LAYERS, PLANE)),
            sem((2, 2)), sem((2, 2)), sem((3, 8)), sem((3, 8)), sem((4,)), sem((4,)),
            sem((PLANE,)), sem((PLANE,)), sem((4,)), sem((4,)), sem((3,)),
            sem((4,)), sem((4,)), sem((4,)), sem((4,)), sem((4, 8)), sem((8,)),
        ],
        compiler_params=pltpu.CompilerParams(
            collective_id=0, has_side_effects=True, vmem_limit_bytes=58 << 20
        ),
        cost_estimate=pl.CostEstimate(flops=3 * 10**9, bytes_accessed=10 * 10**6, transcendentals=4 * 10**6),
    )(ids, shared_ids, query, keys, values, weight)


def on_device(query_rows, key_rows, value_rows, out_weight, random_ids, global_ids):
    tokens, width = query_rows.shape
    blocks = tokens // BLOCK
    rows = [array.reshape(blocks, BLOCK, width) for array in (query_rows, key_rows, value_rows)]
    weight = out_weight.reshape(-1, BLOCK, out_weight.shape[1])
    return gather_attend(random_ids, global_ids, *rows, weight)[0]


def solution(mesh):
    return jax.shard_map(
        on_device,
        mesh=mesh,
        in_specs=(
            P("seq", "fsdp"),
            P("seq", "fsdp"),
            P("seq", "fsdp"),
            P("fsdp", None),
            P("seq", None),
            P(),
        ),
        out_specs=P(("seq", "fsdp"), None),
        check_vma=False,
    )
```

```python
import jax
import jax.numpy as jnp
from jax import lax
from jax.experimental import pallas as pl
from jax.experimental.pallas import tpu as pltpu
from jax.sharding import PartitionSpec as P

HD = 128
BLOCK = 64
G = 2
R = 3
LOW = -1e30
NT = (((1,), (1,)), ((), ()))
MESH = pl.DeviceIdType.MESH
PLANE = 8
LAYERS = 8
SHIFTS = (0, 1, -1, 2, -2, 3, -3, 4)


def lanes_of(parts):
    rows = parts[0].shape[0]
    lane = lax.broadcasted_iota(jnp.int32, (rows, HD), 1)
    out = jnp.zeros((rows, HD), jnp.float32)
    for i, part in enumerate(parts):
        out = jnp.where(lane == i, part, out)
    return out


def kernel(
    ids, shared_ids,
    q_ref, k_ref, v_ref, w_ref,
    out_ref, weight_ref,
    result, heads_in, fetched,
    front1_k, front1_v, back1_k, back1_v, front2_k, front2_v, back2_k, back2_v, stage, pick3, got3, got4,
    halo, key_pad, value_pad, g_mine, g_in, g_part, g_col, g_sum, g_all,
    near_acc, near_max, near_sum, far_acc, far_max, far_sum, context,
    mine_v, inverse_v, table_v, tables_v, inverse, table, tables,
    hop1_s, hop1_r, hop2_s, hop2_r, hop3_s, hop3_r, hop4_s, hop4_r, relay_s, relay_r,
    in_s, in_r, halo_s, halo_r, g_s, g_r, c_s, c_r, t_s, t_r, far_s, far_r, local_s,
    row_s, row_r, core_s, core_r, load_s, out_s,
):
    me = lax.axis_index("seq")
    row = lax.axis_index("fsdp")
    z, p_me = me // PLANE, me % PLANE
    count = PLANE * LAYERS
    tokens, width = key_pad.shape[0] - 2 * BLOCK, q_ref.shape[2]
    heads = width // HD
    pair = 2 * BLOCK

    def col(shift):
        return lax.rem(z + shift + LAYERS, LAYERS) * PLANE + p_me

    def mate(r):
        return lax.rem(p_me + r, PLANE)

    def from_mate(r):
        return lax.rem(p_me - r + PLANE, PLANE)

    def layer(d):
        return lax.rem(z - SHIFTS[d] + LAYERS, LAYERS)

    def copy(src, dst, send, recv, device):
        return pltpu.make_async_remote_copy(
            src_ref=src, dst_ref=dst, send_sem=send, recv_sem=recv,
            device_id={"seq": device}, device_id_type=MESH,
        )

    def cross(src, dst, send, recv, device):
        return pltpu.make_async_remote_copy(
            src_ref=src, dst_ref=dst, send_sem=send, recv_sem=recv,
            device_id={"fsdp": device}, device_id_type=MESH,
        )

    next_one, last_one = lax.rem(me + 1, count), lax.rem(me + count - 1, count)
    barrier = pltpu.get_barrier_semaphore()
    for r in range(1, PLANE):
        pl.semaphore_signal(barrier, inc=1, device_id={"seq": z * PLANE + mate(r)}, device_id_type=MESH)
    for s in range(1, LAYERS):
        pl.semaphore_signal(barrier, inc=1, device_id={"seq": col(s)}, device_id_type=MESH)
    pl.semaphore_signal(barrier, inc=1, device_id={"seq": next_one}, device_id_type=MESH)
    pl.semaphore_signal(barrier, inc=1, device_id={"seq": last_one}, device_id_type=MESH)
    for f in range(1, 4):
        pl.semaphore_signal(barrier, inc=1, device_id={"fsdp": lax.rem(row + f, 4)}, device_id_type=MESH)
    pl.semaphore_wait(barrier, 7 + 7 + 2 + 3)

    ways = (1, -1)
    first_hop = ((front1_k, front1_v), (back1_k, back1_v))
    second_hop = ((front2_k, front2_v), (back2_k, back2_v))
    own = (k_ref, v_ref)

    def hop1(w, t):
        return copy(own[t], first_hop[w][t], hop1_s.at[w, t], hop1_r.at[w, t], col(ways[w]))

    def hop2(w, t):
        return copy(first_hop[w][t], second_hop[w][t], hop2_s.at[w, t], hop2_r.at[w, t], col(ways[w]))

    def hop3(w, t, c):
        part = pl.ds(4 * c, 4)
        return copy(
            pick3.at[w, t, part], got3.at[w, t, part], hop3_s.at[w, t, c], hop3_r.at[w, t, c], col(ways[w])
        )

    def relay(w, t, j):
        return copy(
            got3.at[w, t, j], got4.at[w, t, j], relay_s.at[w, t, j], relay_r.at[w, t, j],
            z * PLANE + mate(2 * j + w),
        )

    def hop4(w, t, j):
        src = got3.at[w, t, j] if 2 * j + w == 0 else got4.at[w, t, j]
        owner = col(-3 * ways[w]) - p_me + from_mate(2 * j + w)
        return copy(src, fetched.at[t, owner], hop4_s.at[w, t, j], hop4_r.at[w, t, j], col(ways[w]))

    def last_arrived(w, t, j):
        spot = fetched.at[t, layer(7) * PLANE + from_mate(2 * j + w)]
        copy(spot, spot, hop4_s.at[w, t, j], hop4_r.at[w, t, j], col(ways[w])).wait_recv()

    core = lax.rem(me, 2)
    depth = w_ref.shape[0]
    part_rows = pl.ds(core * (depth // 2), depth // 2)

    def row_weight(f, at):
        return cross(
            w_ref.at[part_rows], weight_ref.at[at, part_rows], row_s.at[f], row_r.at[f], lax.rem(row + f, 4)
        )

    def core_weight(f, rows):
        came = lax.rem(row - f + 4, 4)
        return copy(
            weight_ref.at[came, rows], weight_ref.at[came, rows], core_s.at[f], core_r.at[f], me + 1 - 2 * core
        )

    other_rows = pl.ds((1 - core) * (depth // 2), depth // 2)
    chunk = 512
    chunks = w_ref.shape[2] // chunk

    def place(k, i):
        if k < 2:
            return (second_hop, first_hop)[k][i // 4][i // 2 % 2].at[pl.ds(depth * (i % 2), depth)]
        if k == 2:
            return stage.at[i // 2, i % 2]
        return (pick3, got3)[i // 4].at[i // 2 % 2, i % 2, pl.ds(0, depth)]

    def load(k, i):
        columns_i = pl.ds(i * chunk, chunk)
        if k == 0:
            src = w_ref.at[:, :, columns_i]
        else:
            src = weight_ref.at[lax.rem(row - k + 4, 4), :, :, columns_i]
        return pltpu.make_async_copy(src, place(k, i), load_s.at[k, i])

    def load_all(k):
        for i in range(chunks):
            load(k, i).start()

    for t in range(2):
        for w in range(2):
            hop1(w, t).start()
    for f in (1, 3, 2):
        row_weight(f, row).start()

    def halo_copy(side, t):
        block = tokens // BLOCK - 1 if side == 0 else 0
        return copy(
            own[t].at[block], halo.at[side, pl.ds(t * BLOCK, BLOCK)], halo_s.at[side, t], halo_r.at[side, t],
            next_one if side == 0 else last_one,
        )

    for side in range(2):
        for t in range(2):
            halo_copy(side, t).start()

    blocks_here = ids.shape[0]
    lane = lax.broadcasted_iota(jnp.int32, mine_v.shape, 1)
    wanted = jnp.zeros(mine_v.shape, jnp.int32)
    askers = jnp.zeros(mine_v.shape, jnp.int32)
    for b in range(blocks_here):
        for j in range(R):
            hit = lane == lax.div(ids[b, j], blocks_here)
            wanted = jnp.where(hit, lax.rem(ids[b, j], blocks_here), wanted)
            askers = jnp.where(hit, b, askers)
    mine_v[...] = wanted
    inverse_v[...] = askers

    def row_copy(r, at):
        return copy(mine_v, table_v.at[at], t_s.at[r], t_r.at[r], z * PLANE + mate(r))

    def table_copy(w, far):
        k = 2 * w + far - 1
        return copy(table_v, tables_v.at[k], far_s.at[k], far_r.at[k], col(-far * ways[w]))

    for r in range(1, PLANE):
        row_copy(r, p_me).start()
    table_v[p_me] = wanted
    keep_inverse = pltpu.make_async_copy(inverse_v, inverse, local_s.at[0])
    keep_table = pltpu.make_async_copy(table_v, table, local_s.at[1])
    keep_tables = pltpu.make_async_copy(tables_v, tables, local_s.at[2])
    keep_inverse.start()

    piece = G * pair // PLANE
    for g in range(G):
        holder = jnp.full((BLOCK, width), lax.div(shared_ids[g], blocks_here), jnp.int32)
        keep = jnp.where(holder == me, 1.0, 0.0)
        for t in range(2):
            block = own[t][lax.rem(shared_ids[g], blocks_here)].astype(jnp.float32) * keep
            g_mine[pl.ds(g * pair + t * BLOCK, BLOCK), :] = block.astype(jnp.bfloat16)

    def piece_at(p):
        return pl.ds(pl.multiple_of(p * piece, piece), piece)

    def g1(r, p):
        return copy(g_mine.at[piece_at(p)], g_in.at[r], g_s.at[0, r], g_r.at[0, r], z * PLANE + p)

    def g2(s):
        return copy(g_part, g_col.at[s], g_s.at[1, s], g_r.at[1, s], col(s))

    def g3(r, p, at):
        return copy(g_sum, g_all.at[piece_at(at)], g_s.at[2, r], g_r.at[2, r], z * PLANE + p)

    def each(low, high, body):
        def step(i, carry):
            body(i)
            return carry

        lax.fori_loop(low, high, step, 0)

    each(1, PLANE, lambda r: g1(r, mate(r)).start())
    g_in[0] = g_mine[piece_at(p_me), :]

    def choose(d, t, read):
        owner = layer(d) * PLANE + p_me

        def one(r):
            stage[d, t, r] = read(table[mate(r), 0, owner])

        each(0, PLANE, one)
        fetched[t, owner] = stage[d, t, 0]

    def spread_one(d, t, r, src):
        owner = layer(d) * PLANE + p_me
        return copy(src, fetched.at[t, owner], in_s.at[t, d, r], in_r.at[t, d, r], z * PLANE + mate(r))

    def spread(d, t):
        each(1, PLANE, lambda r: spread_one(d, t, r, stage.at[d, t, r]).start())

    def arrived(d, r):
        owner = layer(d) * PLANE + from_mate(r)
        for t in range(2):
            spot = fetched.at[t, owner]
            copy(spot, spot, in_s.at[t, d, r], in_r.at[t, d, r], z * PLANE + mate(r)).wait_recv()

    def columns(h):
        return pl.ds(h * HD, HD)

    def attend(owner):
        asker = inverse[0, owner]
        scores = []
        for h in range(heads):
            keys = fetched[0, owner, :, columns(h)]
            scores.append(lax.dot_general(q_ref[asker, :, columns(h)], keys, NT, preferred_element_type=jnp.float32))
        scores = jnp.concatenate(scores, axis=0) * HD**-0.5
        row_max = jnp.max(scores, axis=1, keepdims=True)
        lifted = jnp.exp(scores - row_max)
        row_sum = jnp.sum(lifted, axis=1, keepdims=True)
        lifted = lifted.astype(jnp.bfloat16)
        parts = [slice(h * BLOCK, (h + 1) * BLOCK) for h in range(heads)]
        for h in range(heads):
            values = fetched[1, owner, :, columns(h)]
            far_acc[owner, :, columns(h)] = jnp.dot(lifted[parts[h]], values, preferred_element_type=jnp.float32)
        far_max[owner] = lanes_of([row_max[part] for part in parts])
        far_sum[owner] = lanes_of([row_sum[part] for part in parts])

    def attend_layer(d):
        def one(r):
            @pl.when(r > 0)
            def _():
                arrived(d, r)

            attend(layer(d) * PLANE + from_mate(r))

        each(0, PLANE, one)

    for r in range(1, PLANE):
        row_copy(r, from_mate(r)).wait_recv()
    keep_table.start()
    for w in range(2):
        for far in (1, 2):
            table_copy(w, far).start()
    keep_inverse.wait()
    keep_table.wait()
    for t in range(2):
        choose(0, t, lambda spot: own[t][spot])
        spread(0, t)

    each(1, PLANE, lambda r: g1(r, mate(r)).wait_recv())
    total = g_in[0]
    for r in range(1, PLANE):
        total = total + g_in[r]
    g_part[...] = total
    each(1, LAYERS, lambda s: g2(s).start())
    g_col[0] = total

    attend_layer(0)

    for t in range(2):
        for w in range(2):
            hop1(w, t).wait_recv()
            hop2(w, t).start()
        for w in range(2):
            choose(1 + w, t, lambda spot: first_hop[w][t][spot])
            spread(1 + w, t)

    each(1, LAYERS, lambda s: g2(s).wait_recv())
    total = g_col[0]
    for s in range(1, LAYERS):
        total = total + g_col[s]
    g_sum[...] = total
    each(1, PLANE, lambda r: g3(r, mate(r), p_me).start())
    g_all[piece_at(p_me), :] = total

    for side in range(2):
        for t in range(2):
            halo_copy(side, t).wait_recv()
    pads = (key_pad, value_pad)
    for t in range(2):
        pads[t][pl.ds(0, BLOCK), :] = halo[0, pl.ds(t * BLOCK, BLOCK), :]
        pads[t][pl.ds(BLOCK, tokens), :] = own[t][...].reshape(tokens, width)
        pads[t][pl.ds(BLOCK + tokens, BLOCK), :] = halo[1, pl.ds(t * BLOCK, BLOCK), :]
    each(1, PLANE, lambda r: g3(r, mate(r), from_mate(r)).wait_recv())

    tile = 2 * BLOCK
    span = tile + 2 * BLOCK
    steps = tokens // tile

    def near(step):
        wide = span + G * BLOCK
        row_block = lax.broadcasted_iota(jnp.int32, (tile, wide), 0) // BLOCK
        column = lax.broadcasted_iota(jnp.int32, (tile, wide), 1)
        key_block = column // BLOCK
        first = jnp.where((me == 0) & (step == 0), 1, 0)
        last = jnp.where((me == count - 1) & (step == steps - 1), 1, 0)
        listed = (key_block >= row_block) & (key_block <= row_block + 2)
        listed = listed & (key_block >= first) & (key_block < span // BLOCK - last)
        listed = listed | (column >= span)
        rows = pl.ds(pl.multiple_of(step * tile, tile), tile)
        around = pl.ds(pl.multiple_of(step * tile, tile), span)
        maxima, sums = [], []
        for h in range(heads):
            shared = [g_all[pl.ds(b * BLOCK, BLOCK), columns(h)] for b in range(2 * G)]
            keys = jnp.concatenate([key_pad[around, columns(h)]] + shared[0::2], axis=0)
            values = jnp.concatenate([value_pad[around, columns(h)]] + shared[1::2], axis=0)
            query = q_ref[pl.ds(step * (tile // BLOCK), tile // BLOCK), :, columns(h)].reshape(tile, HD)
            scores = lax.dot_general(query, keys, NT, preferred_element_type=jnp.float32)
            scores = jnp.where(listed, scores * HD**-0.5, LOW)
            row_max = jnp.max(scores, axis=1, keepdims=True)
            lifted = jnp.exp(scores - row_max)
            maxima.append(row_max)
            sums.append(jnp.sum(lifted, axis=1, keepdims=True))
            near_acc[rows, columns(h)] = jnp.dot(
                lifted.astype(jnp.bfloat16), values, preferred_element_type=jnp.float32
            )
        near_max[rows, :] = lanes_of(maxima)
        near_sum[rows, :] = lanes_of(sums)

    each(0, steps, near)
    for w in range(2):
        attend_layer(1 + w)

    for w in range(2):
        for far in (1, 2):
            table_copy(w, far).wait_recv()
    keep_tables.start()
    keep_tables.wait()
    for t in range(2):
        for w in range(2):
            hop2(w, t).wait_recv()
            owner = col(-2 * ways[w])

            def one(j, r, far):
                pick3[w, t, j] = second_hop[w][t][tables[2 * w + far - 1, mate(r), 0, owner]]

            each(0, 4, lambda j: one(j, 2 * j + w, 2))
            hop3(w, t, 0).start()
            each(0, PLANE, lambda r: one(4 + r, r, 1))
            for c in (1, 2):
                hop3(w, t, c).start()
        for w in range(2):
            choose(3 + w, t, lambda spot: second_hop[w][t][spot])
            spread(3 + w, t)
    for t in range(2):
        for w in range(2):
            hop3(w, t, 0).wait_recv()
            for j in range(4):
                (hop4 if 2 * j + w == 0 else relay)(w, t, j).start()
        for c in (1, 2):
            for w in range(2):
                hop3(w, t, c).wait_recv()
                for r in range(4 * c - 4, 4 * c):
                    if r == 0:
                        fetched[t, layer(5 + w) * PLANE + p_me] = got3[w, t, 4]
                    else:
                        spread_one(5 + w, t, r, got3.at[w, t, 4 + r]).start()
            if c == 1:
                for w in range(2):
                    for j in range(4):
                        if 2 * j + w > 0:
                            relay(w, t, j).wait_recv()
                            hop4(w, t, j).start()
        if t == 0:
            for f in (1, 3, 2):
                row_weight(f, lax.rem(row - f + 4, 4)).wait_recv()
                core_weight(f, part_rows).start()
            for w in range(2):
                attend_layer(3 + w)
            load_all(0)
    attend_layer(5)
    attend_layer(6)
    for w in range(2):
        for t in range(2):
            hop2(w, t).wait_send()
    for f in range(1, 4):
        core_weight(f, other_rows).wait_recv()
    load_all(1)
    for d in range(5):
        for t in range(2):
            each(1, PLANE, lambda r: spread_one(d, t, r, fetched.at[t, 0]).wait_send())
    load_all(2)
    for w in range(2):
        for j in range(4):
            for t in range(2):
                last_arrived(w, t, j)
            attend(layer(7) * PLANE + from_mate(2 * j + w))

    quarter = tokens // 4

    def merge(block):
        rows = pl.ds(pl.multiple_of(block * BLOCK, BLOCK), BLOCK)
        slots = [lax.div(ids[block, j], blocks_here) for j in range(R)]
        maxima = [near_max[rows, :]] + [far_max[slot] for slot in slots]
        top = maxima[0]
        for one in maxima[1:]:
            top = jnp.maximum(top, one)
        scales = [jnp.exp(one - top) for one in maxima]
        sums = [near_sum[rows, :]] + [far_sum[slot] for slot in slots]
        whole = scales[0] * sums[0]
        for scale, one in zip(scales[1:], sums[1:]):
            whole = whole + scale * one
        scales = [scale / whole for scale in scales]
        for h in range(heads):
            out = scales[0][:, h : h + 1] * near_acc[rows, columns(h)]
            for scale, slot in zip(scales[1:], slots):
                out = out + scale[:, h : h + 1] * far_acc[slot, :, columns(h)]
            context[rows, columns(h)] = out.astype(jnp.bfloat16)

    def quarter_at(f):
        return pl.ds(pl.multiple_of(f * quarter, quarter), quarter)

    def exchange(f):
        to = lax.rem(row + f, 4)
        return cross(context.at[quarter_at(to)], heads_in.at[f], c_s.at[f], c_r.at[f], to)

    blocks = quarter // BLOCK
    for f in (2, 1, 3, 0):
        to = lax.rem(row + f, 4)
        each(0, blocks, lambda b: merge(to * blocks + b))
        if f > 0:
            exchange(f).start()

    def tile_of(k, i):
        return place(k, i)[...].reshape(depth * BLOCK, chunk)

    for t in range(2):
        for w in range(2):
            for c in range(3):
                hop3(w, t, c).wait_send()
            for j in range(4):
                if 2 * j + w > 0:
                    relay(w, t, j).wait_send()
                else:
                    hop4(w, t, j).wait_send()
            each(1, PLANE, lambda r: spread_one(5 + w, t, r, fetched.at[t, 0]).wait_send())
    load_all(3)

    group = quarter // BLOCK

    def product(block, k, i):
        return jnp.dot(block, tile_of(k, i), preferred_element_type=jnp.float32)

    mine = context[quarter_at(row), :]
    for i in range(chunks):
        load(0, i).wait()
        far_acc[pl.ds(group * i, group)] = product(mine, 0, i).reshape(group, BLOCK, chunk)
    for f in (2, 1, 3):
        exchange(f).wait_recv()

    def write(i):
        columns_i = pl.ds(i * chunk, chunk)
        return pltpu.make_async_copy(result.at[:, columns_i], out_ref.at[:, columns_i], out_s.at[i])

    for i in range(chunks):
        part = far_acc[pl.ds(group * i, group)].reshape(quarter, chunk)
        for f in (1, 2, 3):
            load(f, i).wait()
            part = part + product(heads_in[f], f, i)
        result[:, pl.ds(i * chunk, chunk)] = part.astype(jnp.bfloat16)
        write(i).start()

    for t in range(2):
        for w in range(2):
            hop1(w, t).wait_send()
            for j in range(4):
                if 2 * j + w > 0:
                    hop4(w, t, j).wait_send()
    for side in range(2):
        for t in range(2):
            halo_copy(side, t).wait_send()
    each(1, PLANE, lambda r: g1(r, mate(r)).wait_send())
    each(1, LAYERS, lambda s: g2(s).wait_send())
    each(1, PLANE, lambda r: g3(r, mate(r), p_me).wait_send())
    for r in range(1, PLANE):
        row_copy(r, p_me).wait_send()
    for w in range(2):
        for far in (1, 2):
            table_copy(w, far).wait_send()
    for f in range(1, 4):
        row_weight(f, row).wait_send()
        core_weight(f, part_rows).wait_send()
        exchange(f).wait_send()
    for i in range(chunks):
        write(i).wait()


def gather_attend(ids, shared_ids, query, keys, values, weight):
    tokens, width = query.shape[0] * BLOCK, query.shape[2]
    n = PLANE * LAYERS
    pair = 2 * BLOCK
    piece = G * pair // PLANE
    half, full = jnp.bfloat16, jnp.float32
    vmem = pl.BlockSpec(memory_space=pltpu.VMEM)
    smem = pl.BlockSpec(memory_space=pltpu.SMEM)
    sem = pltpu.SemaphoreType.DMA
    hop = pltpu.VMEM(query.shape, half)
    return pl.pallas_call(
        kernel,
        out_shape=[
            jax.ShapeDtypeStruct((tokens // 4, weight.shape[2]), half),
            jax.ShapeDtypeStruct((4,) + weight.shape, half),
        ],
        in_specs=[smem] * 2 + [vmem] * 3 + [pl.BlockSpec(memory_space=pl.ANY)],
        out_specs=[pl.BlockSpec(memory_space=pl.ANY)] * 2,
        scratch_shapes=[
            pltpu.VMEM((tokens // 4, weight.shape[2]), half),
            pltpu.VMEM((4, tokens // 4, width), half),
            pltpu.VMEM((2, n, BLOCK, width), half),
            hop, hop, hop, hop, hop, hop, hop, hop,
            pltpu.VMEM((5, 2, PLANE, BLOCK, width), half),
            pltpu.VMEM((2, 2, 12, BLOCK, width), half),
            pltpu.VMEM((2, 2, 12, BLOCK, width), half),
            pltpu.VMEM((2, 2, 4, BLOCK, width), half),
            pltpu.VMEM((2, pair, width), half),
            pltpu.VMEM((tokens + pair, width), half),
            pltpu.VMEM((tokens + pair, width), half),
            pltpu.VMEM((G * pair, width), half),
            pltpu.VMEM((PLANE, piece, width), half),
            pltpu.VMEM((piece, width), half),
            pltpu.VMEM((LAYERS, piece, width), half),
            pltpu.VMEM((piece, width), half),
            pltpu.VMEM((G * pair, width), half),
            pltpu.VMEM((tokens, width), full),
            pltpu.VMEM((tokens, HD), full),
            pltpu.VMEM((tokens, HD), full),
            pltpu.VMEM((n, BLOCK, width), full),
            pltpu.VMEM((n, BLOCK, HD), full),
            pltpu.VMEM((n, BLOCK, HD), full),
            pltpu.VMEM((tokens, width), half),
            pltpu.VMEM((PLANE, HD), jnp.int32),
            pltpu.VMEM((PLANE, HD), jnp.int32),
            pltpu.VMEM((PLANE, PLANE, HD), jnp.int32),
            pltpu.VMEM((4, PLANE, PLANE, HD), jnp.int32),
            pltpu.SMEM((PLANE, HD), jnp.int32),
            pltpu.SMEM((PLANE, PLANE, HD), jnp.int32),
            pltpu.SMEM((4, PLANE, PLANE, HD), jnp.int32),
            sem((2, 2)), sem((2, 2)), sem((2, 2)), sem((2, 2)),
            sem((2, 2, 3)), sem((2, 2, 3)), sem((2, 2, 4)), sem((2, 2, 4)), sem((2, 2, 4)), sem((2, 2, 4)),
            sem((2, LAYERS, PLANE)), sem((2, LAYERS, PLANE)),
            sem((2, 2)), sem((2, 2)), sem((3, 8)), sem((3, 8)), sem((4,)), sem((4,)),
            sem((PLANE,)), sem((PLANE,)), sem((4,)), sem((4,)), sem((3,)),
            sem((4,)), sem((4,)), sem((4,)), sem((4,)), sem((4, 8)), sem((8,)),
        ],
        compiler_params=pltpu.CompilerParams(
            collective_id=0, has_side_effects=True, vmem_limit_bytes=58 << 20
        ),
        cost_estimate=pl.CostEstimate(flops=3 * 10**9, bytes_accessed=10 * 10**6, transcendentals=4 * 10**6),
    )(ids, shared_ids, query, keys, values, weight)


def on_device(query_rows, key_rows, value_rows, out_weight, random_ids, global_ids):
    tokens, width = query_rows.shape
    blocks = tokens // BLOCK
    rows = [array.reshape(blocks, BLOCK, width) for array in (query_rows, key_rows, value_rows)]
    weight = out_weight.reshape(-1, BLOCK, out_weight.shape[1])
    return gather_attend(random_ids, global_ids, *rows, weight)[0]


def solution(mesh):
    return jax.shard_map(
        on_device,
        mesh=mesh,
        in_specs=(
            P("seq", "fsdp"),
            P("seq", "fsdp"),
            P("seq", "fsdp"),
            P("fsdp", None),
            P("seq", None),
            P(),
        ),
        out_specs=P(("seq", "fsdp"), None),
        check_vma=False,
    )
```
